256 devices in a mesh: step: 4 (over x), node: 64 (over z, y, core).
Axes of the slice: x: 4, y: 4, z: 8, core: 2. Of those that a mesh axis runs over, the one named last changes fastest.
Arguments:
- states: bfloat16 [4, 16384, 512], P('step', 'node'), may hold values from -16 to 16
- step_cotangents: float32 [4, 16384, 512], P('step', 'node'), may hold values from -6 to 6
- weights: bfloat16 [512, 3072], replicated, may hold values from -0.25 to 0.25
- edge_tiles: bfloat16 [64, 16, 128, 128], P('node'), may hold values from -0.1875 to 0.1875
- tile_src: int32 [64, 16], P('node'), may hold values from 0 to 5, as said below
- tile_dst: int32 [64, 16], P('node'), may hold values from 0 to 1
- tile_counts: int32 [64], P('node'), may hold values from 4 to 16, as said below
Outputs:
- state_adjoints: float32 [4, 16384, 512], P('step', 'node')
- weight_grads: float32 [512, 3072], P('node')
The draws below stay inside these ranges and needn't reach their ends.
Inputs may be any that keep to these rules, and one draw needn't show every extreme that they name: `tile_src`: slot 0 of every device names a block below 2 and slot 1 one from 4. `tile_counts`: some device has all 16 slots live.
All inputs are finite; a program needn't handle non-finite values.
Results may differ from the reference program's by a relative error of at most 0.029.
Values may be sent and summed in bfloat16 or wider, within the bound.
No kernel may reach another device: no remote copies, remote signals or barrier semaphores. Data moves between devices by JAX's collectives and lax.ppermute only.
A program may use at most 128 MiB of HBM per device.

```python
import math
import jax
import jax.numpy as jnp
from jax import lax

D = 512
LAYERS = 2
BLK = 128
NBLK = 2
TILES_MAX = 16
NODES = 16384
N_STEP = 4
N_NODE = 64


def draw_tile_src(key, part):
    key = jax.random.fold_in(key, 11)
    key_base, key_left, key_right = jax.random.split(key, 3)
    base = jax.random.randint(key_base, (N_NODE, TILES_MAX), 0, 3 * NBLK)
    left = jax.random.randint(key_left, (N_NODE,), 0, NBLK)
    right = jax.random.randint(key_right, (N_NODE,), 2 * NBLK, 3 * NBLK)
    slots = jnp.arange(TILES_MAX)[None, :]
    result = jnp.where(slots == 0, left[:, None], base)
    result = jnp.where(slots == 1, right[:, None], result)
    return result.astype(jnp.int32)


def draw_tile_counts(key, part):
    key = jax.random.fold_in(key, 12)
    key_counts, key_pick = jax.random.split(key, 2)
    counts = jax.random.randint(key_counts, (N_NODE,), max(2, TILES_MAX // 4), TILES_MAX + 1)
    chosen = jax.random.randint(key_pick, (), 0, N_NODE)
    counts = jnp.where(jnp.arange(N_NODE) == chosen, TILES_MAX, counts)
    return counts.astype(jnp.int32)


def plant(entries, stream_key, least, largest):
    place = [jax.random.randint(jax.random.fold_in(stream_key, axis), (), 0, length) for axis, length in enumerate(entries.shape)]
    main_axis = entries.shape.index(max(entries.shape))
    next_to = place[:main_axis] + [(place[main_axis] + 1) % entries.shape[main_axis]] + place[main_axis + 1:]
    return entries.at[tuple(place)].set(least).at[tuple(next_to)].set(largest)


def with_spikes(array, own_key, source, target, shards_of, factor):
    owner, partner = [(jnp.arange(array.shape[dim]) // (array.shape[dim] // shards_of)).reshape([-1 if axis == dim else 1 for axis in range(array.ndim)]) for dim in (source, target)]
    chosen = jax.random.permutation(own_key, shards_of)[partner]
    strong = (owner == chosen) | (owner == (partner + shards_of // 2) % shards_of)
    return jnp.where(strong, factor * array, array)


def level_of(stream_key, extent, pieces, smallest, top_value):
    def one(axis_at, parts):
        draws = jax.random.uniform(jax.random.fold_in(jax.random.fold_in(stream_key, 6), axis_at), (parts,), jnp.float32, smallest / len(pieces), top_value / len(pieces))
        return jnp.repeat(jnp.exp(draws), extent[axis_at] // parts).reshape((-1,) + (1,) * (len(extent) - axis_at - 1))

    loudness = one(*pieces[0])
    for cut in pieces[1:]:
        loudness = loudness * one(*cut)
    return loudness


def centred(key, extent, width, most, shards=(), kind=jnp.bfloat16):
    drawn = jax.random.normal(key, extent, jnp.float32) * width
    if len(shards) > 0:
        drawn = level_of(key, extent, shards, -0.22, 0.18) * drawn
    return jnp.clip(drawn, min=-most, max=most).astype(kind)


def gaussian_with(own_key, dims, width, limit, cuts, heavy, dtype=jnp.bfloat16):
    entries = width * jax.random.normal(own_key, dims, jnp.float32)
    if cuts:
        entries = entries * level_of(own_key, dims, cuts, -0.22, 0.18)
    return jnp.clip(with_spikes(entries, jax.random.fold_in(own_key, 3), *heavy), -limit, limit).astype(dtype)


def setup_inputs(seed: int = 0) -> dict:
    streams_of = jax.random.split(jax.random.key(seed), 8)
    return {
        "states": gaussian_with(streams_of[0], (N_STEP, NODES, D), 1.0, 16.0, ((0, 4), (1, 64)), (1, 2, 64, 4.0)),
        "step_cotangents": centred(streams_of[1], (N_STEP, NODES, D), 1.0, 6.0, ((0, 4), (1, 64)), jnp.float32),
        "weights": centred(streams_of[2], (D, 3 * LAYERS * D), D ** -0.5, 0.25),
        "edge_tiles": centred(streams_of[3], (N_NODE, TILES_MAX, BLK, BLK), (BLK * TILES_MAX // NBLK) ** -0.5, 0.1875, ((0, 64),)),
        "tile_src": draw_tile_src(jax.random.fold_in(streams_of[7], 71), 0),
        "tile_dst": plant(jax.random.randint(streams_of[5], (N_NODE, TILES_MAX), 0, NBLK), jax.random.fold_in(streams_of[5], 1), 0, NBLK - 1).astype(jnp.int32),
        "tile_counts": draw_tile_counts(jax.random.fold_in(streams_of[7], 71), 0),
    }


def silu_slope(z):
    sig = jax.nn.sigmoid(z)
    return sig * (1.0 + z * (1.0 - sig))

def pick_blocks(blocks, index):
    return jax.vmap(lambda b, i: b[i])(blocks, index)

def neighbourhood(x):
    return jnp.concatenate([jnp.roll(x, 1, axis=0), x, jnp.roll(x, -1, axis=0)], axis=1)

def reference(states, step_cotangents, weights, edge_tiles, tile_src, tile_dst, tile_counts):
    devs = N_NODE
    rows = NBLK * BLK
    live = jnp.arange(TILES_MAX)[None, :] < tile_counts[:, None]
    dst_hot = ((tile_dst[:, None, :] == jnp.arange(NBLK)[None, :, None]) & live[:, None, :]).astype(jnp.float32)
    src_hot = ((tile_src[:, None, :] == jnp.arange(3 * NBLK)[None, :, None]) & live[:, None, :]).astype(jnp.float32)
    tiles32 = edge_tiles.astype(jnp.float32)
    total = jnp.zeros((D, 3 * LAYERS * D), jnp.float32)
    adjoints = []
    incoming = jnp.zeros((devs, rows, D), jnp.float32)
    for s in range(N_STEP - 1, -1, -1):
        h = states[s].reshape(devs, rows, D).astype(jnp.float32)
        saved = []
        for layer in range(LAYERS):
            base = 3 * layer * D
            wa = weights[:, base:base + D]
            wb = weights[:, base + D:base + 2 * D]
            wc = weights[:, base + 2 * D:base + 3 * D]
            hb = h.astype(jnp.bfloat16)
            blocks = neighbourhood(hb).reshape(devs, 3 * NBLK, BLK, D)
            sel = pick_blocks(blocks, tile_src).astype(jnp.float32)
            prod = jnp.einsum('ptij,ptjd->ptid', tiles32, sel)
            m = jnp.einsum('pbt,ptid->pbid', dst_hot, prod, precision=lax.Precision.HIGHEST)
            mb = m.reshape(devs * rows, D).astype(jnp.bfloat16)
            hb2 = hb.reshape(devs * rows, D)
            z = jnp.dot(hb2, wa, preferred_element_type=jnp.float32) + jnp.dot(mb, wb, preferred_element_type=jnp.float32)
            g = jax.nn.silu(z).astype(jnp.bfloat16)
            h = h + jnp.dot(g, wc, preferred_element_type=jnp.float32).reshape(devs, rows, D)
            saved.append((hb2, mb, z, g))
        a = step_cotangents[s].reshape(devs, rows, D) + incoming
        grads = [None] * LAYERS
        for layer in range(LAYERS - 1, -1, -1):
            base = 3 * layer * D
            wa = weights[:, base:base + D]
            wb = weights[:, base + D:base + 2 * D]
            wc = weights[:, base + 2 * D:base + 3 * D]
            hb2, mb, z, g = saved[layer]
            ab = a.reshape(devs * rows, D).astype(jnp.bfloat16)
            dz = jnp.dot(ab, wc.T, preferred_element_type=jnp.float32) * silu_slope(z)
            dzb = dz.astype(jnp.bfloat16)
            dm = jnp.dot(dzb, wb.T, preferred_element_type=jnp.float32).astype(jnp.bfloat16)
            local = a + jnp.dot(dzb, wa.T, preferred_element_type=jnp.float32).reshape(devs, rows, D)
            dsel = pick_blocks(dm.reshape(devs, NBLK, BLK, D), tile_dst).astype(jnp.float32)
            contrib = jnp.einsum('ptji,ptjd->ptid', tiles32, dsel)
            cpad = jnp.einsum('pct,ptid->pcid', src_hot, contrib, precision=lax.Precision.HIGHEST).reshape(devs, 3 * rows, D)
            a = local + cpad[:, rows:2 * rows] + jnp.roll(cpad[:, :rows], -1, axis=0) + jnp.roll(cpad[:, 2 * rows:], 1, axis=0)
            grads[layer] = jnp.concatenate([jnp.dot(hb2.T, dzb, preferred_element_type=jnp.float32), jnp.dot(mb.T, dzb, preferred_element_type=jnp.float32), jnp.dot(g.T, ab, preferred_element_type=jnp.float32)], axis=1)
        total = total + jnp.concatenate(grads, axis=1)
        adjoints.append(a.reshape(devs * rows, D))
        incoming = a
    state_adjoints = jnp.stack(adjoints[::-1], axis=0)
    scale = 1.0 / math.sqrt(N_STEP * NODES)
    return (state_adjoints, total * scale)
```

```python
import math

import jax
import jax.numpy as jnp
from jax import lax
from jax.sharding import PartitionSpec as P

Z, Y, C = 8, 4, 2
NODES = Z * Y * C
STEPS = 4
F32 = jnp.float32
BF16 = jnp.bfloat16


def place(z, y, c):
    return (z * Y + y) * C + c


def split(p):
    return p // (Y * C), (p // C) % Y, p % C


def snake(p):
    z, y, c = split(p)
    return place(z, y if z % 2 == 0 else Y - 1 - y, c)


def beyond(q):
    return (q + 1) % NODES if q % 2 else (q - 1) % NODES


DEVICES = range(NODES)
FLIP = [(snake(p), p) for p in DEVICES]
OUTER = [(p, snake(beyond(snake(p)))) for p in DEVICES]
OUTER_HOME = [(beyond(snake(p)), p) for p in DEVICES]
SIBLING = [(p, p ^ 1) for p in DEVICES]
Z_GROUPS = [[place(z, y, c) for z in range(Z)] for y in range(Y) for c in range(C)]


def over_node(value, pairs):
    return lax.ppermute(value, "node", pairs)


def over_step(value, k):
    return lax.ppermute(value, "step", [(s, s ^ k) for s in range(STEPS)])


def over_both(value, k):
    pairs = [((s ^ k) * NODES + snake(p), s * NODES + p) for s in range(STEPS) for p in DEVICES]
    return lax.ppermute(value, ("step", "node"), pairs)


def y_pairs(k):
    return [(place(z, y, c), place(z, y ^ k, c)) for z in range(Z) for y in range(Y) for c in range(C)]


def pick(slots, k):
    low = (k & 1) == 1
    first = jnp.where(low, slots[1], slots[0])
    second = jnp.where(low, slots[3], slots[2])
    return jnp.where((k & 2) == 2, second, first)


def mul(left, right):
    return jnp.dot(left, right, preferred_element_type=F32)


def mul_t(left, right):
    return lax.dot_general(left, right, (((1,), (1,)), ((), ())), preferred_element_type=F32)


def t_mul(left, right):
    return lax.dot_general(left, right, (((0,), (0,)), ((), ())), preferred_element_type=F32)


def assemble(tiles, sources, targets, count, core, nblk):
    slots, block = tiles.shape[0], tiles.shape[1]
    third = sources // nblk
    third = jnp.where(core == 1, 2 - third, third)
    column = third * nblk + sources % nblk
    cell = targets * (3 * nblk) + column
    live = jnp.arange(slots) < count
    hot = ((cell[None, :] == jnp.arange(3 * nblk * nblk)[:, None]) & live[None, :]).astype(BF16)
    blocks = lax.dot_general(hot, tiles, (((1,), (0,)), ((), ())), preferred_element_type=F32)
    blocks = blocks.astype(BF16).reshape(nblk, 3 * nblk, block, block)
    return blocks.transpose(0, 2, 1, 3).reshape(nblk * block, 3 * nblk * block)


def feature_order(width):
    per = width // NODES // STEPS
    order = []
    for s in range(STEPS):
        for c in range(C):
            for y in range(Y):
                for z in range(Z):
                    for r in range(per):
                        order.append(place(z, y, c) * per * STEPS + s * per + r)
    return order


def on_device(states, step_cotangents, weights, edge_tiles, tile_src, tile_dst, tile_counts):
    rows, width = states.shape[1], states.shape[2]
    layers = weights.shape[1] // (3 * width)
    nblk = rows // edge_tiles.shape[2]
    me = lax.axis_index("node")
    x = lax.axis_index("step")
    zi, yi, ci = split(me)
    w = [
        [weights[:, (3 * layer + j) * width : (3 * layer + j + 1) * width] for j in range(3)]
        for layer in range(layers)
    ]

    home = states[0]
    hb = over_node(home, FLIP)
    outer = over_node(home, OUTER_HOME)
    matrix = assemble(edge_tiles[0], tile_src[0], tile_dst[0], tile_counts[0], ci, nblk)
    matrix = over_node(matrix, FLIP)
    m_out, m_own, m_sib = (matrix[:, j * rows : (j + 1) * rows] for j in range(3))
    cot = step_cotangents[0].astype(BF16)
    cots = [over_both(cot, k) for k in range(STEPS)]

    h = hb.astype(F32)
    left_hand, slopes = [], []
    for layer in range(layers):
        wa, wb, wc = w[layer]
        if layer:
            hb = h.astype(BF16)
            outer = over_node(hb, OUTER)
        sib = over_node(hb, SIBLING)
        mb = (mul(m_own, hb) + mul(m_sib, sib) + mul(m_out, outer)).astype(BF16)
        zz = mul(hb, wa) + mul(mb, wb)
        sig = jax.nn.sigmoid(zz)
        g = (zz * sig).astype(BF16)
        slopes.append((sig * (1.0 + zz * (1.0 - sig))).astype(BF16))
        left_hand.append((hb, mb, g))
        if layer + 1 < layers:
            h = h + mul(g, wc)

    slope_slots = [None] * layers
    for layer in range(layers - 1, -1, -1):
        v = slopes[layer]
        slope_slots[layer] = [v] + [over_step(v, k) for k in range(1, STEPS)]
    n_out = over_node(m_out, OUTER)
    n_sib = over_node(m_sib, SIBLING)

    quarter = width // STEPS
    order = feature_order(width)
    perm = jnp.arange(width)[:, None] == jnp.asarray(order)[None, :]
    perm = perm.astype(BF16)
    ordered = [
        mul(v, perm).astype(BF16).reshape(rows, STEPS, quarter) for three in left_hand for v in three
    ]
    ordered = jnp.concatenate(ordered, axis=2)
    lhs_slots = []
    for k in range(STEPS):
        part = lax.dynamic_index_in_dim(ordered, x ^ k, 1, keepdims=False)
        lhs_slots.append(over_step(part, k) if k else part)

    adjoint = jnp.zeros((rows, width), F32)
    result = jnp.zeros((rows, width), F32)
    grads = [[0.0, 0.0] for layer in range(layers)]
    for s in range(STEPS - 1, -1, -1):
        adjoint = adjoint + pick(cots, x ^ s).astype(F32)
        lhs = pick(lhs_slots, x ^ s)
        for layer in range(layers - 1, -1, -1):
            wa, wb, wc = w[layer]
            ab = adjoint.astype(BF16)
            dzb = (mul_t(ab, wc) * pick(slope_slots[layer], x ^ s).astype(F32)).astype(BF16)
            dm = mul_t(dzb, wb).astype(BF16)
            d_out = over_node(dm, OUTER)
            d_sib = over_node(dm, SIBLING)
            adjoint = adjoint + mul_t(dzb, wa) + t_mul(m_own, dm)
            adjoint = adjoint + t_mul(n_sib, d_sib) + t_mul(n_out, d_out)
            base = 3 * layer * quarter
            grads[layer][0] += t_mul(lhs[:, base : base + 2 * quarter], dzb)
            grads[layer][1] += t_mul(lhs[:, base + 2 * quarter : base + 3 * quarter], ab)
        result = jnp.where(x == s, adjoint, result)
    result = over_node(result.astype(BF16), FLIP).astype(F32)

    pieces = []
    for layer in range(layers):
        both, last = grads[layer]
        pieces += [both[:quarter], both[quarter:], last]
    grad = jnp.concatenate(pieces, axis=1)
    half = quarter // C
    sent = lax.dynamic_slice_in_dim(grad, (1 - ci) * half, half, 0).astype(BF16)
    grad = lax.dynamic_slice_in_dim(grad, ci * half, half, 0) + over_node(sent, SIBLING).astype(F32)
    chunk = half // Y
    grad_b = grad.astype(BF16)
    total = lax.dynamic_slice_in_dim(grad, yi * chunk, chunk, 0)
    for k in range(1, Y):
        sent = lax.dynamic_slice_in_dim(grad_b, (yi ^ k) * chunk, chunk, 0)
        total = total + over_node(sent, y_pairs(k)).astype(F32)
    sent = total.astype(BF16).reshape(Z, chunk // Z, -1)
    got = lax.all_to_all(sent, "node", 0, 0, axis_index_groups=Z_GROUPS, tiled=False)
    mine = jnp.sum(got.astype(F32), axis=0)
    mine = mine.astype(BF16)
    slots = [mine] + [over_step(mine, k) for k in range(1, STEPS)]
    share = jnp.concatenate([pick(slots, x ^ s) for s in range(STEPS)], axis=0).astype(F32)
    scale = 1.0 / math.sqrt(STEPS * rows * NODES)
    return (result[None], share * scale)


def solution(mesh):
    return jax.shard_map(
        on_device,
        mesh=mesh,
        in_specs=(
            P("step", "node", None),
            P("step", "node", None),
            P(),
            P("node", None, None, None),
            P("node", None),
            P("node", None),
            P("node"),
        ),
        out_specs=(P("step", "node", None), P("node", None)),
        check_vma=False,
    )
```

```python
import math

import jax
import jax.numpy as jnp
from jax import lax
from jax.sharding import PartitionSpec as P

Z, Y, C = 8, 4, 2
NODES = Z * Y * C
STEPS = 4
F32 = jnp.float32
BF16 = jnp.bfloat16


def place(z, y, c):
    return (z * Y + y) * C + c


def split(p):
    return p // (Y * C), (p // C) % Y, p % C


def snake(p):
    z, y, c = split(p)
    return place(z, y if z % 2 == 0 else Y - 1 - y, c)


def beyond(q):
    return (q + 1) % NODES if q % 2 else (q - 1) % NODES


DEVICES = range(NODES)
FLIP = [(snake(p), p) for p in DEVICES]
OUTER = [(p, snake(beyond(snake(p)))) for p in DEVICES]
OUTER_HOME = [(beyond(snake(p)), p) for p in DEVICES]
SIBLING = [(p, p ^ 1) for p in DEVICES]
Z_GROUPS = [[place(z, y, c) for z in range(Z)] for y in range(Y) for c in range(C)]


def over_node(value, pairs):
    return lax.ppermute(value, "node", pairs)


def over_step(value, k):
    return lax.ppermute(value, "step", [(s, s ^ k) for s in range(STEPS)])


def over_both(value, k):
    pairs = [((s ^ k) * NODES + snake(p), s * NODES + p) for s in range(STEPS) for p in DEVICES]
    return lax.ppermute(value, ("step", "node"), pairs)


def y_pairs(k):
    return [(place(z, y, c), place(z, y ^ k, c)) for z in range(Z) for y in range(Y) for c in range(C)]


def pick(slots, k):
    low = (k & 1) == 1
    first = jnp.where(low, slots[1], slots[0])
    second = jnp.where(low, slots[3], slots[2])
    return jnp.where((k & 2) == 2, second, first)


def mul(left, right):
    return jnp.dot(left, right, preferred_element_type=F32)


def mul_t(left, right):
    return lax.dot_general(left, right, (((1,), (1,)), ((), ())), preferred_element_type=F32)


def t_mul(left, right):
    return lax.dot_general(left, right, (((0,), (0,)), ((), ())), preferred_element_type=F32)


def assemble(tiles, sources, targets, count, core, nblk):
    slots, block = tiles.shape[0], tiles.shape[1]
    third = sources // nblk
    third = jnp.where(core == 1, 2 - third, third)
    column = third * nblk + sources % nblk
    cell = targets * (3 * nblk) + column
    live = jnp.arange(slots) < count
    hot = ((cell[None, :] == jnp.arange(3 * nblk * nblk)[:, None]) & live[None, :]).astype(BF16)
    blocks = lax.dot_general(hot, tiles, (((1,), (0,)), ((), ())), preferred_element_type=F32)
    blocks = blocks.astype(BF16).reshape(nblk, 3 * nblk, block, block)
    return blocks.transpose(0, 2, 1, 3).reshape(nblk * block, 3 * nblk * block)


def feature_choice(width, x, per):
    column = lax.broadcasted_iota(jnp.int32, (width, width), 1)
    row = lax.broadcasted_iota(jnp.int32, (width, width), 0)
    pair = column % per
    rest = column // per
    z, rest = rest % Z, rest // Z
    y, rest = rest % Y, rest // Y
    c, k = rest % C, rest // C
    feature = place(z, y, c) * (per * STEPS) + (x ^ k) * per + pair
    return (row == feature).astype(BF16)


def after(value, *others):
    return lax.optimization_barrier((value, *others))[0]


def on_device(states, step_cotangents, weights, edge_tiles, tile_src, tile_dst, tile_counts):
    rows, width = states.shape[1], states.shape[2]
    layers = weights.shape[1] // (3 * width)
    nblk = rows // edge_tiles.shape[2]
    me = lax.axis_index("node")
    x = lax.axis_index("step")
    zi, yi, ci = split(me)
    w = [
        [weights[:, (3 * layer + j) * width : (3 * layer + j + 1) * width] for j in range(3)]
        for layer in range(layers)
    ]

    home = states[0]
    hb = over_node(home, FLIP)
    outer = over_node(home, OUTER_HOME)
    matrix = assemble(edge_tiles[0], tile_src[0], tile_dst[0], tile_counts[0], ci, nblk)
    cot = after(step_cotangents[0], matrix).astype(BF16)
    matrix = over_node(matrix, FLIP)
    m_out, m_own, m_sib = (matrix[:, j * rows : (j + 1) * rows] for j in range(3))
    cot = over_node(cot, FLIP)

    h = hb.astype(F32)
    left_hand, slope_slots = [], []
    for layer in range(layers):
        wa, wb, wc = w[layer]
        if layer:
            hb = h.astype(BF16)
            outer = over_node(hb, OUTER)
        sib = over_node(hb, SIBLING)
        local = mul(m_own, hb)
        first = mul(hb, wa)
        mb = (local + mul(m_sib, sib) + mul(m_out, outer)).astype(BF16)
        zz = first + mul(mb, wb)
        sig = jax.nn.sigmoid(zz)
        g = (zz * sig).astype(BF16)
        slope = (sig * (1.0 + zz * (1.0 - sig))).astype(BF16)
        if layer + 1 < layers:
            h = h + mul(g, wc)
            slope = after(slope, h)
        slope_slots.append([slope] + [over_step(slope, k) for k in (1, 3, 2)])
        left_hand += [hb, mb, g]
    slope_slots = [[v[0], v[1], v[3], v[2]] for v in slope_slots]
    cot = after(cot, left_hand[3])
    cots = [cot, over_step(cot, 1), over_step(cot, 2), over_step(cot, 3)]
    n_out = over_node(m_out, OUTER)
    n_sib = over_node(m_sib, SIBLING)

    quarter = width // STEPS
    choice = feature_choice(width, x, width // NODES // STEPS)
    ordered = [mul(v, choice).astype(BF16) for v in after(tuple(left_hand), slope_slots[-1][0])]

    def share_left_hand(tie):
        parts = []
        for k in range(STEPS):
            part = [v[:, k * quarter : (k + 1) * quarter] for v in ordered]
            parts.append(jnp.concatenate(part, axis=1))
        parts = lax.optimization_barrier((tie, *parts))[1:]
        return [parts[0]] + [over_step(parts[k], k) for k in range(1, STEPS)]

    adjoint = None
    result = jnp.zeros((rows, width), F32)
    grads = [[0.0, 0.0] for layer in range(layers)]
    kept = {}
    lhs_slots = None
    for s in range(STEPS - 1, -1, -1):
        cot = pick(cots, x ^ s)
        if adjoint is None:
            adjoint = cot.astype(F32)
        else:
            adjoint = adjoint + after(cot, dm).astype(F32)
        for layer in range(layers - 1, -1, -1):
            wa, wb, wc = w[layer]
            ab = adjoint.astype(BF16)
            dzb = (mul_t(ab, wc) * pick(slope_slots[layer], x ^ s).astype(F32)).astype(BF16)
            dm = mul_t(dzb, wb).astype(BF16)
            kept[s, layer] = (ab, dzb)
            d_out = over_node(dm, OUTER)
            adjoint = adjoint + mul_t(dzb, wa) + t_mul(m_own, dm)
            d_sib = over_node(after(dm, adjoint), SIBLING)
            if lhs_slots is None:
                lhs_slots = share_left_hand(dm)
            elif s < STEPS - 1:
                grads[layer] = add_grads(grads[layer], pick(lhs_slots, x ^ (s + 1)), kept[s + 1, layer], layer, dm)
            adjoint = adjoint + t_mul(n_sib, d_sib) + t_mul(n_out, d_out)
        result = jnp.where(x == s, adjoint, result)
    for layer in range(layers - 1, -1, -1):
        grads[layer] = add_grads(grads[layer], pick(lhs_slots, x), kept[0, layer], layer)
    result = over_node(result.astype(BF16), FLIP).astype(F32)

    pieces = []
    for layer in range(layers):
        both, last = grads[layer]
        pieces += [both[:quarter], both[quarter:], last]
    grad = jnp.concatenate(pieces, axis=1)
    half = quarter // C
    sent = lax.dynamic_slice_in_dim(grad, (1 - ci) * half, half, 0).astype(BF16)
    grad = lax.dynamic_slice_in_dim(grad, ci * half, half, 0) + over_node(sent, SIBLING).astype(F32)
    chunk = half // Y
    grad_b = grad.astype(BF16)
    total = lax.dynamic_slice_in_dim(grad, yi * chunk, chunk, 0)
    for k in range(1, Y):
        sent = lax.dynamic_slice_in_dim(grad_b, (yi ^ k) * chunk, chunk, 0)
        total = total + over_node(sent, y_pairs(k)).astype(F32)
    sent = total.astype(BF16).reshape(Z, chunk // Z, -1)
    got = lax.all_to_all(sent, "node", 0, 0, axis_index_groups=Z_GROUPS, tiled=False)
    mine = jnp.sum(got.astype(F32), axis=0)
    mine = mine.astype(BF16)
    slots = [mine] + [over_step(mine, k) for k in range(1, STEPS)]
    share = jnp.concatenate([pick(slots, x ^ s) for s in range(STEPS)], axis=0).astype(F32)
    scale = 1.0 / math.sqrt(STEPS * rows * NODES)
    return (result[None], share * scale)


def add_grads(sums, lhs, pair, layer, tie=None):
    quarter = lhs.shape[1] // 6
    ab, dzb = pair
    if tie is not None:
        ab, dzb = after(ab, tie), after(dzb, tie)
    base = 3 * layer * quarter
    both = t_mul(lhs[:, base : base + 2 * quarter], dzb)
    last = t_mul(lhs[:, base + 2 * quarter : base + 3 * quarter], ab)
    return [sums[0] + both, sums[1] + last]


def solution(mesh):
    return jax.shard_map(
        on_device,
        mesh=mesh,
        in_specs=(
            P("step", "node", None),
            P("step", "node", None),
            P(),
            P("node", None, None, None),
            P("node", None),
            P("node", None),
            P("node"),
        ),
        out_specs=(P("step", "node", None), P("node", None)),
        check_vma=False,
    )
```

```python
import math

import jax
import jax.numpy as jnp
from jax import lax
from jax.sharding import PartitionSpec as P

Z, Y, C = 8, 4, 2
NODES = Z * Y * C
STEPS = 4
F32 = jnp.float32
BF16 = jnp.bfloat16


def place(z, y, c):
    return (z * Y + y) * C + c


def split(p):
    return p // (Y * C), (p // C) % Y, p % C


def snake(p):
    z, y, c = split(p)
    return place(z, y if z % 2 == 0 else Y - 1 - y, c)


def beyond(q):
    return (q + 1) % NODES if q % 2 else (q - 1) % NODES


DEVICES = range(NODES)
FLIP = [(snake(p), p) for p in DEVICES]
OUTER = [(p, snake(beyond(snake(p)))) for p in DEVICES]
OUTER_NATURAL = [(p, beyond(p)) for p in DEVICES]
OUTER_HOME = [(beyond(snake(p)), p) for p in DEVICES]
SIBLING = [(p, p ^ 1) for p in DEVICES]
Z_GROUPS = [[place(z, y, c) for z in range(Z)] for y in range(Y) for c in range(C)]


def over_node(value, pairs):
    return lax.ppermute(value, "node", pairs)


def over_step(value, k):
    return lax.ppermute(value, "step", [(s, s ^ k) for s in range(STEPS)])


def over_both(value, k):
    pairs = [((s ^ k) * NODES + snake(p), s * NODES + p) for s in range(STEPS) for p in DEVICES]
    return lax.ppermute(value, ("step", "node"), pairs)


def y_pairs(k):
    return [(place(z, y, c), place(z, y ^ k, c)) for z in range(Z) for y in range(Y) for c in range(C)]


def pick(slots, k):
    low = (k & 1) == 1
    first = jnp.where(low, slots[1], slots[0])
    second = jnp.where(low, slots[3], slots[2])
    return jnp.where((k & 2) == 2, second, first)


def mul(left, right):
    return jnp.dot(left, right, preferred_element_type=F32)


def mul_t(left, right):
    return lax.dot_general(left, right, (((1,), (1,)), ((), ())), preferred_element_type=F32)


def t_mul(left, right):
    return lax.dot_general(left, right, (((0,), (0,)), ((), ())), preferred_element_type=F32)


def assemble(tiles, sources, targets, count, core, nblk):
    slots, block = tiles.shape[0], tiles.shape[1]
    third = sources // nblk
    third = jnp.where(core == 1, 2 - third, third)
    column = third * nblk + sources % nblk
    cell = targets * (3 * nblk) + column
    live = jnp.arange(slots) < count
    hot = ((cell[None, :] == jnp.arange(3 * nblk * nblk)[:, None]) & live[None, :]).astype(BF16)
    blocks = lax.dot_general(hot, tiles, (((1,), (0,)), ((), ())), preferred_element_type=F32)
    blocks = blocks.astype(BF16).reshape(nblk, 3 * nblk, block, block)
    return blocks.transpose(0, 2, 1, 3).reshape(nblk * block, 3 * nblk * block)


def feature_choice(width, x, per):
    column = lax.broadcasted_iota(jnp.int32, (width, width), 1)
    row = lax.broadcasted_iota(jnp.int32, (width, width), 0)
    pair = column % per
    rest = column // per
    z, rest = rest % Z, rest // Z
    y, rest = rest % Y, rest // Y
    c, k = rest % C, rest // C
    feature = place(z, y, c) * (per * STEPS) + (x ^ k) * per + pair
    return (row == feature).astype(BF16)


def forward(hb, outer, sib, matrix, weights):
    wa, wb, _ = weights
    rows = hb.shape[0]
    m_out, m_own, m_sib = (matrix[:, j * rows : (j + 1) * rows] for j in range(3))
    local = mul(m_own, hb)
    first = mul(hb, wa)
    mb = (local + mul(m_sib, sib) + mul(m_out, outer)).astype(BF16)
    z = first + mul(mb, wb)
    sig = jax.nn.sigmoid(z)
    return mb, (z * sig).astype(BF16), (sig * (1.0 + z * (1.0 - sig))).astype(BF16)


def after(value, *others):
    return lax.optimization_barrier((value, *others))[0]


def on_device(states, step_cotangents, weights, edge_tiles, tile_src, tile_dst, tile_counts):
    rows, width = states.shape[1], states.shape[2]
    layers = weights.shape[1] // (3 * width)
    nblk = rows // edge_tiles.shape[2]
    me = lax.axis_index("node")
    x = lax.axis_index("step")
    zi, yi, ci = split(me)
    w = [
        [weights[:, (3 * layer + j) * width : (3 * layer + j + 1) * width] for j in range(3)]
        for layer in range(layers)
    ]

    home = states[0]
    outer = over_node(home, OUTER_NATURAL)
    sib = over_node(home, SIBLING)
    matrix_home = assemble(edge_tiles[0], tile_src[0], tile_dst[0], tile_counts[0], ci, nblk)
    cot = after(step_cotangents[0], matrix_home).astype(BF16)
    matrix = over_node(matrix_home, FLIP)
    cot = over_node(cot, FLIP)
    h = home.astype(F32) + mul(forward(home, outer, sib, matrix_home, w[0])[1], w[0][2])
    moved = h.astype(BF16)
    hb = over_node(moved, FLIP)
    outer = over_node(moved, OUTER_HOME)
    home = after(home, moved)
    hb_0 = over_node(home, FLIP)
    outer_0 = over_node(home, OUTER_HOME)
    sib = over_node(hb, SIBLING)
    cot = after(cot, moved)
    cots = [cot, over_step(cot, 1), over_step(cot, 2), over_step(cot, 3)]
    n_out = over_node(matrix[:, :rows], OUTER)
    n_sib = over_node(matrix[:, 2 * rows :], SIBLING)
    m_own = matrix[:, rows : 2 * rows]

    mb, g, slope = forward(hb, outer, sib, matrix, w[1])
    slots_1 = [slope] + [over_step(slope, k) for k in (1, 2, 3)]
    hb_0, outer_0 = lax.optimization_barrier((hb_0, outer_0, slope))[:2]
    sib_0 = over_node(hb_0, SIBLING)
    mb_0, g_0, slope_0 = forward(hb_0, outer_0, sib_0, matrix, w[0])
    slots_0 = [slope_0] + [over_step(slope_0, k) for k in (1, 2, 3)]
    slope_slots = [slots_0, slots_1]

    quarter = width // STEPS
    choice = feature_choice(width, x, width // NODES // STEPS)
    left_hand = after((hb_0, mb_0, g_0, hb, mb, g), slope_0)
    ordered = [mul(v, choice).astype(BF16) for v in left_hand]
    parts = []
    for k in range(STEPS):
        part = [v[:, k * quarter : (k + 1) * quarter] for v in ordered]
        parts.append(jnp.concatenate(part, axis=1))
    lhs_slots = [parts[0], None, None, None]
    crossing = {(3, 0): 1, (2, 1): 3, (2, 0): 2}
    formed = {(1, 1): [(3, 1), (2, 1)], (1, 0): [(3, 0), (2, 0)], (0, 1): [(1, 1)], (0, 0): [(1, 0), (0, 1)]}

    adjoint = None
    result = jnp.zeros((rows, width), F32)
    grads = [[0.0, 0.0] for layer in range(layers)]
    kept = {}
    for s in range(STEPS - 1, -1, -1):
        cot = pick(cots, x ^ s)
        if adjoint is None:
            adjoint = after(cot, slope).astype(F32)
        else:
            adjoint = adjoint + after(cot, dm).astype(F32)
        for layer in range(layers - 1, -1, -1):
            wa, wb, wc = w[layer]
            ab = adjoint.astype(BF16)
            dzb = (mul_t(ab, wc) * pick(slope_slots[layer], x ^ s).astype(F32)).astype(BF16)
            dm = mul_t(dzb, wb).astype(BF16)
            kept[s, layer] = (ab, dzb)
            d_out = over_node(dm, OUTER)
            adjoint = adjoint + mul_t(dzb, wa) + t_mul(m_own, dm)
            d_sib = over_node(after(dm, adjoint), SIBLING)
            if (s, layer) in crossing:
                k = crossing[s, layer]
                lhs_slots[k] = over_step(after(parts[k], dm), k)
            for other in formed.get((s, layer), ()):
                lhs = pick(lhs_slots, x ^ other[0])
                grads[other[1]] = add_grads(grads[other[1]], lhs, kept[other], other[1], dm)
            adjoint = adjoint + t_mul(n_sib, d_sib) + t_mul(n_out, d_out)
        result = jnp.where(x == s, adjoint, result)
    grads[0] = add_grads(grads[0], pick(lhs_slots, x), kept[0, 0], 0)

    pieces = []
    for layer in range(layers):
        both, last = grads[layer]
        pieces += [both[:quarter], both[quarter:], last]
    grad = jnp.concatenate(pieces, axis=1)
    half = quarter // C
    sent = lax.dynamic_slice_in_dim(grad, (1 - ci) * half, half, 0).astype(BF16)
    grad = lax.dynamic_slice_in_dim(grad, ci * half, half, 0) + over_node(sent, SIBLING).astype(F32)
    chunk = half // Y
    grad_b = grad.astype(BF16)
    total = lax.dynamic_slice_in_dim(grad, yi * chunk, chunk, 0)
    for k in range(1, Y):
        sent = lax.dynamic_slice_in_dim(grad_b, (yi ^ k) * chunk, chunk, 0)
        total = total + over_node(sent, y_pairs(k)).astype(F32)
    sent = total.astype(BF16).reshape(Z, chunk // Z, -1)
    result = over_node(after(result, sent).astype(BF16), FLIP).astype(F32)
    got = lax.all_to_all(sent, "node", 0, 0, axis_index_groups=Z_GROUPS, tiled=False)
    mine = jnp.sum(got.astype(F32), axis=0)
    mine = mine.astype(BF16)
    slots = [mine] + [over_step(mine, k) for k in range(1, STEPS)]
    share = jnp.concatenate([pick(slots, x ^ s) for s in range(STEPS)], axis=0).astype(F32)
    scale = 1.0 / math.sqrt(STEPS * rows * NODES)
    return (result[None], share * scale)


def add_grads(sums, lhs, pair, layer, tie=None):
    quarter = lhs.shape[1] // 6
    ab, dzb = pair
    if tie is not None:
        ab, dzb = after(ab, tie), after(dzb, tie)
    base = 3 * layer * quarter
    both = t_mul(lhs[:, base : base + 2 * quarter], dzb)
    last = t_mul(lhs[:, base + 2 * quarter : base + 3 * quarter], ab)
    return [sums[0] + both, sums[1] + last]


def solution(mesh):
    return jax.shard_map(
        on_device,
        mesh=mesh,
        in_specs=(
            P("step", "node", None),
            P("step", "node", None),
            P(),
            P("node", None, None, None),
            P("node", None),
            P("node", None),
            P("node"),
        ),
        out_specs=(P("step", "node", None), P("node", None)),
        check_vma=False,
    )
```

```python
import math

import jax
import jax.numpy as jnp
from jax import lax
from jax.sharding import PartitionSpec as P

Z, Y, C = 8, 4, 2
NODES = Z * Y * C
STEPS = 4
F32 = jnp.float32
BF16 = jnp.bfloat16


def place(z, y, c):
    return (z * Y + y) * C + c


def split(p):
    return p // (Y * C), (p // C) % Y, p % C


def snake(p):
    z, y, c = split(p)
    return place(z, y if z % 2 == 0 else Y - 1 - y, c)


def beyond(q):
    return (q + 1) % NODES if q % 2 else (q - 1) % NODES


DEVICES = range(NODES)
FLIP = [(snake(p), p) for p in DEVICES]
OUTER = [(p, snake(beyond(snake(p)))) for p in DEVICES]
OUTER_HOME = [(beyond(snake(p)), p) for p in DEVICES]
SIBLING = [(p, p ^ 1) for p in DEVICES]
Z_GROUPS = [[place(z, y, c) for z in range(Z)] for y in range(Y) for c in range(C)]


def over_node(value, pairs):
    return lax.ppermute(value, "node", pairs)


def over_step(value, k):
    return lax.ppermute(value, "step", [(s, s ^ k) for s in range(STEPS)])


def over_both(value, k):
    pairs = [((s ^ k) * NODES + snake(p), s * NODES + p) for s in range(STEPS) for p in DEVICES]
    return lax.ppermute(value, ("step", "node"), pairs)


def y_pairs(k):
    return [(place(z, y, c), place(z, y ^ k, c)) for z in range(Z) for y in range(Y) for c in range(C)]


def pick(slots, k):
    low = (k & 1) == 1
    first = jnp.where(low, slots[1], slots[0])
    second = jnp.where(low, slots[3], slots[2])
    return jnp.where((k & 2) == 2, second, first)


def mul(left, right):
    return jnp.dot(left, right, preferred_element_type=F32)


def mul_t(left, right):
    return lax.dot_general(left, right, (((1,), (1,)), ((), ())), preferred_element_type=F32)


def t_mul(left, right):
    return lax.dot_general(left, right, (((0,), (0,)), ((), ())), preferred_element_type=F32)


def assemble(tiles, sources, targets, count, core, nblk):
    slots, block = tiles.shape[0], tiles.shape[1]
    third = sources // nblk
    third = jnp.where(core == 1, 2 - third, third)
    column = third * nblk + sources % nblk
    cell = targets * (3 * nblk) + column
    live = jnp.arange(slots) < count
    hot = ((cell[None, :] == jnp.arange(3 * nblk * nblk)[:, None]) & live[None, :]).astype(BF16)
    blocks = lax.dot_general(hot, tiles, (((1,), (0,)), ((), ())), preferred_element_type=F32)
    blocks = blocks.astype(BF16).reshape(nblk, 3 * nblk, block, block)
    return blocks.transpose(0, 2, 1, 3).reshape(nblk * block, 3 * nblk * block)


def feature_choice(width, x, per):
    column = lax.broadcasted_iota(jnp.int32, (width, width), 1)
    row = lax.broadcasted_iota(jnp.int32, (width, width), 0)
    pair = column % per
    rest = column // per
    z, rest = rest % Z, rest // Z
    y, rest = rest % Y, rest // Y
    c, k = rest % C, rest // C
    feature = place(z, y, c) * (per * STEPS) + (x ^ k) * per + pair
    return (row == feature).astype(BF16)


def after(value, *others):
    return lax.optimization_barrier((value, *others))[0]


def on_device(states, step_cotangents, weights, edge_tiles, tile_src, tile_dst, tile_counts):
    rows, width = states.shape[1], states.shape[2]
    layers = weights.shape[1] // (3 * width)
    nblk = rows // edge_tiles.shape[2]
    me = lax.axis_index("node")
    x = lax.axis_index("step")
    zi, yi, ci = split(me)
    w = [
        [weights[:, (3 * layer + j) * width : (3 * layer + j + 1) * width] for j in range(3)]
        for layer in range(layers)
    ]

    home = states[0]
    hb = over_node(home, FLIP)
    outer = over_node(home, OUTER_HOME)
    matrix = assemble(edge_tiles[0], tile_src[0], tile_dst[0], tile_counts[0], ci, nblk)
    cot = after(step_cotangents[0], matrix).astype(BF16)
    matrix = over_node(matrix, FLIP)
    m_out, m_own, m_sib = (matrix[:, j * rows : (j + 1) * rows] for j in range(3))
    cots = [cot] + [over_step(cot, k) for k in (1, 2, 3)]

    h = hb.astype(F32)
    left_hand, slope_slots = [], []
    for layer in range(layers):
        wa, wb, wc = w[layer]
        if layer:
            hb = h.astype(BF16)
            outer = over_node(hb, OUTER)
        sib = over_node(hb, SIBLING)
        local = mul(m_own, hb)
        first = mul(hb, wa)
        mb = (local + mul(m_sib, sib) + mul(m_out, outer)).astype(BF16)
        zz = first + mul(mb, wb)
        sig = jax.nn.sigmoid(zz)
        g = (zz * sig).astype(BF16)
        slope = (sig * (1.0 + zz * (1.0 - sig))).astype(BF16)
        if layer + 1 < layers:
            h = h + mul(g, wc)
            slope = after(slope, h)
        slope_slots.append([slope] + [over_step(slope, k) for k in (1, 2, 3)])
        left_hand += [hb, mb, g]
    n_out = over_node(m_out, OUTER)
    n_sib = over_node(m_sib, SIBLING)
    cot_next = over_node(after(pick(cots, x ^ (STEPS - 1)), left_hand[3]), FLIP)

    quarter = width // STEPS
    choice = feature_choice(width, x, width // NODES // STEPS)
    lhs_slots = [None] * STEPS
    crossing = {(3, 0): 1, (2, 1): 3, (2, 0): 2}
    arrived = {(2, 0): 1, (1, 1): 3, (1, 0): 2}
    formed = {(1, 0): [(3, 1), (2, 1)], (0, 1): [(3, 0), (2, 0), (1, 1)], (0, 0): [(1, 0), (0, 1)]}

    adjoint = None
    result = jnp.zeros((rows, width), F32)
    grads = [[0.0, 0.0] for layer in range(layers)]
    kept = {}
    for s in range(STEPS - 1, -1, -1):
        cot = cot_next.astype(F32)
        adjoint = cot if adjoint is None else adjoint + cot
        for layer in range(layers - 1, -1, -1):
            wa, wb, wc = w[layer]
            ab = adjoint.astype(BF16)
            dzb = (mul_t(ab, wc) * pick(slope_slots[layer], x ^ s).astype(F32)).astype(BF16)
            dm = mul_t(dzb, wb).astype(BF16)
            kept[s, layer] = (ab, dzb)
            if (s, layer) in arrived:
                k = arrived[s, layer]
                dm, lhs_slots[k] = lax.optimization_barrier((dm, lhs_slots[k]))
            d_out = over_node(dm, OUTER)
            adjoint = adjoint + mul_t(dzb, wa) + t_mul(m_own, dm)
            d_sib = over_node(after(dm, adjoint), SIBLING)
            if s == STEPS - 1 and layer == layers - 1:
                ordered = [mul(v, choice).astype(BF16) for v in after(tuple(left_hand), dm)]
                parts = []
                for k in range(STEPS):
                    part = [v[:, k * quarter : (k + 1) * quarter] for v in ordered]
                    parts.append(jnp.concatenate(part, axis=1))
                lhs_slots[0] = parts[0]
            if (s, layer) in crossing:
                k = crossing[s, layer]
                lhs_slots[k] = over_step(after(parts[k], dm), k)
            if s and layer == layers - 1:
                cot_next = over_node(after(pick(cots, x ^ (s - 1)), dm), FLIP)
            for other in formed.get((s, layer), ()):
                lhs = pick(lhs_slots, x ^ other[0])
                grads[other[1]] = add_grads(grads[other[1]], lhs, kept[other], other[1], dm)
            adjoint = adjoint + t_mul(n_sib, d_sib) + t_mul(n_out, d_out)
        result = jnp.where(x == s, adjoint, result)
    grads[0] = add_grads(grads[0], pick(lhs_slots, x), kept[0, 0], 0)

    pieces = []
    for layer in range(layers):
        both, last = grads[layer]
        pieces += [both[:quarter], both[quarter:], last]
    grad = jnp.concatenate(pieces, axis=1)
    half = quarter // C
    sent = lax.dynamic_slice_in_dim(grad, (1 - ci) * half, half, 0).astype(BF16)
    grad = lax.dynamic_slice_in_dim(grad, ci * half, half, 0) + over_node(sent, SIBLING).astype(F32)
    chunk = half // Y
    grad_b = grad.astype(BF16)
    total = lax.dynamic_slice_in_dim(grad, yi * chunk, chunk, 0)
    for k in range(1, Y):
        sent = lax.dynamic_slice_in_dim(grad_b, (yi ^ k) * chunk, chunk, 0)
        total = total + over_node(sent, y_pairs(k)).astype(F32)
    sent = total.astype(BF16).reshape(Z, chunk // Z, -1)
    result = over_node(after(result, sent).astype(BF16), FLIP).astype(F32)
    got = lax.all_to_all(sent, "node", 0, 0, axis_index_groups=Z_GROUPS, tiled=False)
    mine = jnp.sum(got.astype(F32), axis=0)
    mine = mine.astype(BF16)
    slots = [mine] + [over_step(mine, k) for k in range(1, STEPS)]
    share = jnp.concatenate([pick(slots, x ^ s) for s in range(STEPS)], axis=0).astype(F32)
    scale = 1.0 / math.sqrt(STEPS * rows * NODES)
    return (result[None], share * scale)


def add_grads(sums, lhs, pair, layer, tie=None):
    quarter = lhs.shape[1] // 6
    ab, dzb = pair
    if tie is not None:
        ab, dzb = after(ab, tie), after(dzb, tie)
    base = 3 * layer * quarter
    both = t_mul(lhs[:, base : base + 2 * quarter], dzb)
    last = t_mul(lhs[:, base + 2 * quarter : base + 3 * quarter], ab)
    return [sums[0] + both, sums[1] + last]


def solution(mesh):
    return jax.shard_map(
        on_device,
        mesh=mesh,
        in_specs=(
            P("step", "node", None),
            P("step", "node", None),
            P(),
            P("node", None, None, None),
            P("node", None),
            P("node", None),
            P("node"),
        ),
        out_specs=(P("step", "node", None), P("node", None)),
        check_vma=False,
    )
```

```python
import math

import jax
import jax.numpy as jnp
from jax import lax
from jax.sharding import PartitionSpec as P

Z, Y, C = 8, 4, 2
NODES = Z * Y * C
STEPS = 4
SPLIT = 2
F32 = jnp.float32
BF16 = jnp.bfloat16


def place(z, y, c):
    return (z * Y + y) * C + c


def split(p):
    return p // (Y * C), (p // C) % Y, p % C


def snake(p):
    z, y, c = split(p)
    return place(z, y if z % 2 == 0 else Y - 1 - y, c)


def beyond(q):
    return (q + 1) % NODES if q % 2 else (q - 1) % NODES


DEVICES = range(NODES)
FLIP = [(snake(p), p) for p in DEVICES]
OUTER = [(p, snake(beyond(snake(p)))) for p in DEVICES]
OUTER_HOME = [(beyond(snake(p)), p) for p in DEVICES]
SIBLING = [(p, p ^ 1) for p in DEVICES]
Z_GROUPS = [[place(z, y, c) for z in range(Z)] for y in range(Y) for c in range(C)]


def over_node(value, pairs):
    return lax.ppermute(value, "node", pairs)


def over_step(value, k):
    return lax.ppermute(value, "step", [(s, s ^ k) for s in range(STEPS)])


def over_both(value, k):
    pairs = [((s ^ k) * NODES + snake(p), s * NODES + p) for s in range(STEPS) for p in DEVICES]
    return lax.ppermute(value, ("step", "node"), pairs)


def y_pairs(k):
    return [(place(z, y, c), place(z, y ^ k, c)) for z in range(Z) for y in range(Y) for c in range(C)]


def mul(left, right):
    return jnp.dot(left, right, preferred_element_type=F32)


def mul_t(left, right):
    return lax.dot_general(left, right, (((1,), (1,)), ((), ())), preferred_element_type=F32)


def t_mul(left, right):
    return lax.dot_general(left, right, (((0,), (0,)), ((), ())), preferred_element_type=F32)


def assemble(tiles, sources, targets, count, core, nblk):
    slots, block = tiles.shape[0], tiles.shape[1]
    third = sources // nblk
    third = jnp.where(core == 1, 2 - third, third)
    column = third * nblk + sources % nblk
    cell = targets * (3 * nblk) + column
    live = jnp.arange(slots) < count
    hot = ((cell[None, :] == jnp.arange(3 * nblk * nblk)[:, None]) & live[None, :]).astype(BF16)
    blocks = lax.dot_general(hot, tiles, (((1,), (0,)), ((), ())), preferred_element_type=F32)
    blocks = blocks.astype(BF16).reshape(nblk, 3 * nblk, block, block)
    return blocks.transpose(0, 2, 1, 3).reshape(nblk * block, 3 * nblk * block)


def feature_choice(width, x, per):
    column = lax.broadcasted_iota(jnp.int32, (width, width), 1)
    row = lax.broadcasted_iota(jnp.int32, (width, width), 0)
    row_of = column % per
    rest = column // per
    z, rest = rest % Z, rest // Z
    y, rest = rest % Y, rest // Y
    c, k = rest % C, rest // C
    feature = place(z, y, c) * (per * SPLIT) + ((x & 1) ^ k) * per + row_of
    return (row == feature).astype(BF16)


def after(value, *others):
    return lax.optimization_barrier((value, *others))[0]


def on_device(states, step_cotangents, weights, edge_tiles, tile_src, tile_dst, tile_counts):
    rows, width = states.shape[1], states.shape[2]
    layers = weights.shape[1] // (3 * width)
    nblk = rows // edge_tiles.shape[2]
    me = lax.axis_index("node")
    x = lax.axis_index("step")
    zi, yi, ci = split(me)
    w = [
        [weights[:, (3 * layer + j) * width : (3 * layer + j + 1) * width] for j in range(3)]
        for layer in range(layers)
    ]

    home = states[0]
    hb = over_node(home, FLIP)
    outer = over_node(home, OUTER_HOME)
    matrix = assemble(edge_tiles[0], tile_src[0], tile_dst[0], tile_counts[0], ci, nblk)
    cot = after(step_cotangents[0], matrix).astype(BF16)
    matrix = over_node(matrix, FLIP)
    m_out, m_own, m_sib = (matrix[:, j * rows : (j + 1) * rows] for j in range(3))
    cot = over_node(cot, FLIP)

    h = hb.astype(F32)
    left_hand, slopes = [], []
    for layer in range(layers):
        wa, wb, wc = w[layer]
        if layer:
            hb = h.astype(BF16)
            outer = over_node(hb, OUTER)
        sib = over_node(hb, SIBLING)
        local = mul(m_own, hb)
        first = mul(hb, wa)
        mb = (local + mul(m_sib, sib) + mul(m_out, outer)).astype(BF16)
        zz = first + mul(mb, wb)
        sig = jax.nn.sigmoid(zz)
        g = (zz * sig).astype(BF16)
        slope = (sig * (1.0 + zz * (1.0 - sig))).astype(BF16)
        if layer + 1 < layers:
            h = h + mul(g, wc)
            slope = after(slope, h)
        slopes.append((slope, over_step(slope, 1)))
        left_hand += [hb, mb, g]
    cot = after(cot, left_hand[3])
    cots = (cot, over_step(cot, 1))
    n_out = over_node(m_out, OUTER)
    n_sib = over_node(m_sib, SIBLING)

    own_first = (x & 1) == 1

    def of_turn(pair, turn):
        own, other = pair
        return jnp.where(own_first, other, own) if turn % 2 else jnp.where(own_first, own, other)

    upper = x >= 2
    share = width // SPLIT
    choice = feature_choice(width, x, width // NODES // SPLIT)
    adjoint = None
    result = jnp.zeros((rows, width), F32)
    grads = [[0.0, 0.0] for layer in range(layers)]
    kept = {}
    for turn in range(STEPS):
        cot = of_turn(cots, turn).astype(F32)
        if turn == 0:
            adjoint = cot
        elif turn == 2:
            adjoint = cot + over_step(adjoint.astype(BF16), 3).astype(F32)
        else:
            adjoint = adjoint + cot
        for layer in range(layers - 1, -1, -1):
            wa, wb, wc = w[layer]
            ab = adjoint.astype(BF16)
            dzb = (mul_t(ab, wc) * of_turn(slopes[layer], turn).astype(F32)).astype(BF16)
            dm = mul_t(dzb, wb).astype(BF16)
            kept[turn, layer] = (ab, dzb)
            d_out = over_node(dm, OUTER)
            adjoint = adjoint + mul_t(dzb, wa) + t_mul(m_own, dm)
            d_sib = over_node(after(dm, adjoint), SIBLING)
            if turn == 0 and layer == layers - 1:
                ordered = [mul(v, choice).astype(BF16) for v in after(tuple(left_hand), dm)]
                parts = [
                    jnp.concatenate([v[:, k * share : (k + 1) * share] for v in ordered], axis=1)
                    for k in range(SPLIT)
                ]
            if turn == 0 and layer == 0:
                lhs = (parts[0], over_step(after(parts[1], dm), 1))
            if turn >= 2:
                early = kept[turn - 2, layer]
                pair = [jnp.where(upper, e, v) for e, v in zip(early, after((ab, dzb), dm))]
                grads[layer] = add_grads(grads[layer], of_turn(lhs, turn), pair, layer)
            adjoint = adjoint + t_mul(n_sib, d_sib) + t_mul(n_out, d_out)
        result = jnp.where(x == STEPS - 1 - turn, adjoint, result)
    result = over_node(result.astype(BF16), FLIP).astype(F32)

    pieces = []
    for layer in range(layers):
        both, last = grads[layer]
        pieces += [both[:share], both[share:], last]
    grad = jnp.concatenate(pieces, axis=1)
    half = share // C
    sent = lax.dynamic_slice_in_dim(grad, (1 - ci) * half, half, 0).astype(BF16)
    grad = lax.dynamic_slice_in_dim(grad, ci * half, half, 0) + over_node(sent, SIBLING).astype(F32)
    chunk = half // Y
    grad_b = grad.astype(BF16)
    total = lax.dynamic_slice_in_dim(grad, yi * chunk, chunk, 0)
    for k in range(1, Y):
        sent = lax.dynamic_slice_in_dim(grad_b, (yi ^ k) * chunk, chunk, 0)
        total = total + over_node(sent, y_pairs(k)).astype(F32)
    sent = total.astype(BF16).reshape(Z, chunk // Z, -1)
    got = lax.all_to_all(sent, "node", 0, 0, axis_index_groups=Z_GROUPS, tiled=False)
    mine = jnp.sum(got.astype(F32), axis=0).astype(BF16)
    beside, same, across = [over_step(mine, k).astype(F32) for k in (1, 2, 3)]
    mine, beside = mine.astype(F32) + same, beside + across
    low = jnp.where(own_first, beside, mine)
    high = jnp.where(own_first, mine, beside)
    scale = 1.0 / math.sqrt(STEPS * rows * NODES)
    return (result[None], jnp.concatenate([low, high], axis=0) * scale)


def add_grads(sums, lhs, pair, layer):
    share = lhs.shape[1] // 6
    ab, dzb = pair
    base = 3 * layer * share
    both = t_mul(lhs[:, base : base + 2 * share], dzb)
    last = t_mul(lhs[:, base + 2 * share : base + 3 * share], ab)
    return [sums[0] + both, sums[1] + last]


def solution(mesh):
    return jax.shard_map(
        on_device,
        mesh=mesh,
        in_specs=(
            P("step", "node", None),
            P("step", "node", None),
            P(),
            P("node", None, None, None),
            P("node", None),
            P("node", None),
            P("node"),
        ),
        out_specs=(P("step", "node", None), P("node", None)),
        check_vma=False,
    )
```

```python
import math

import jax
import jax.numpy as jnp
from jax import lax
from jax.sharding import PartitionSpec as P

Z, Y, C = 8, 4, 2
NODES = Z * Y * C
STEPS = 4
SPLIT = 2
F32 = jnp.float32
BF16 = jnp.bfloat16


def place(z, y, c):
    return (z * Y + y) * C + c


def split(p):
    return p // (Y * C), (p // C) % Y, p % C


def snake(p):
    z, y, c = split(p)
    return place(z, y if z % 2 == 0 else Y - 1 - y, c)


def beyond(q):
    return (q + 1) % NODES if q % 2 else (q - 1) % NODES


DEVICES = range(NODES)
FLIP = [(snake(p), p) for p in DEVICES]
OUTER = [(p, snake(beyond(snake(p)))) for p in DEVICES]
OUTER_HOME = [(beyond(snake(p)), p) for p in DEVICES]
SIBLING = [(p, p ^ 1) for p in DEVICES]
Z_GROUPS = [[place(z, y, c) for z in range(Z)] for y in range(Y) for c in range(C)]


def over_node(value, pairs):
    return lax.ppermute(value, "node", pairs)


def over_step(value, k):
    return lax.ppermute(value, "step", [(s, s ^ k) for s in range(STEPS)])


def over_both(value, k):
    pairs = [((s ^ k) * NODES + snake(p), s * NODES + p) for s in range(STEPS) for p in DEVICES]
    return lax.ppermute(value, ("step", "node"), pairs)


def y_pairs(k):
    return [(place(z, y, c), place(z, y ^ k, c)) for z in range(Z) for y in range(Y) for c in range(C)]


def mul(left, right):
    return jnp.dot(left, right, preferred_element_type=F32)


def mul_t(left, right):
    return lax.dot_general(left, right, (((1,), (1,)), ((), ())), preferred_element_type=F32)


def t_mul(left, right):
    return lax.dot_general(left, right, (((0,), (0,)), ((), ())), preferred_element_type=F32)


def assemble(tiles, sources, targets, count, core, nblk):
    slots, block = tiles.shape[0], tiles.shape[1]
    third = sources // nblk
    third = jnp.where(core == 1, 2 - third, third)
    column = third * nblk + sources % nblk
    cell = targets * (3 * nblk) + column
    live = jnp.arange(slots) < count
    hot = ((cell[None, :] == jnp.arange(3 * nblk * nblk)[:, None]) & live[None, :]).astype(BF16)
    blocks = lax.dot_general(hot, tiles, (((1,), (0,)), ((), ())), preferred_element_type=F32)
    blocks = blocks.astype(BF16).reshape(nblk, 3 * nblk, block, block)
    return blocks.transpose(0, 2, 1, 3).reshape(nblk * block, 3 * nblk * block)


def feature_choice(width, x, yi, ci, per):
    column = lax.broadcasted_iota(jnp.int32, (width, width), 1)
    row = lax.broadcasted_iota(jnp.int32, (width, width), 0)
    row_of = column % per
    rest = column // per
    z, rest = rest % Z, rest // Z
    y, rest = rest % Y, rest // Y
    c, k = rest % C, rest // C
    feature = place(z, y ^ yi, c ^ ci) * (per * SPLIT) + ((x & 1) ^ k) * per + row_of
    return (row == feature).astype(BF16)


def after(value, *others):
    return lax.optimization_barrier((value, *others))[0]


def on_device(states, step_cotangents, weights, edge_tiles, tile_src, tile_dst, tile_counts):
    rows, width = states.shape[1], states.shape[2]
    layers = weights.shape[1] // (3 * width)
    nblk = rows // edge_tiles.shape[2]
    me = lax.axis_index("node")
    x = lax.axis_index("step")
    zi, yi, ci = split(me)
    w = [
        [weights[:, (3 * layer + j) * width : (3 * layer + j + 1) * width] for j in range(3)]
        for layer in range(layers)
    ]

    home = states[0]
    hb = over_node(home, FLIP)
    outer = over_node(home, OUTER_HOME)
    matrix = assemble(edge_tiles[0], tile_src[0], tile_dst[0], tile_counts[0], ci, nblk)
    cot = after(step_cotangents[0], matrix).astype(BF16)
    matrix = over_node(matrix, FLIP)
    m_out, m_own, m_sib = (matrix[:, j * rows : (j + 1) * rows] for j in range(3))
    cot = over_node(cot, FLIP)

    h = hb.astype(F32)
    left_hand, slopes = [], []
    for layer in range(layers):
        wa, wb, wc = w[layer]
        if layer:
            hb = h.astype(BF16)
            outer = over_node(hb, OUTER)
        sib = over_node(hb, SIBLING)
        local = mul(m_own, hb)
        first = mul(hb, wa)
        mb = (local + mul(m_sib, sib) + mul(m_out, outer)).astype(BF16)
        zz = first + mul(mb, wb)
        sig = jax.nn.sigmoid(zz)
        g = (zz * sig).astype(BF16)
        slope = (sig * (1.0 + zz * (1.0 - sig))).astype(BF16)
        if layer + 1 < layers:
            h = h + mul(g, wc)
            slope = after(slope, h)
        slopes.append((slope, over_step(slope, 1)))
        left_hand += [hb, mb, g]
    cot = after(cot, left_hand[3])
    cots = (cot, over_step(cot, 1))
    n_out = over_node(m_out, OUTER)
    n_sib = over_node(m_sib, SIBLING)

    own_first = (x & 1) == 1

    def of_turn(pair, turn):
        own, other = pair
        return jnp.where(own_first, other, own) if turn % 2 else jnp.where(own_first, own, other)

    upper = x >= 2
    share = width // SPLIT
    choice = feature_choice(width, x, yi, ci, width // NODES // SPLIT)
    adjoint = None
    result = jnp.zeros((rows, width), F32)
    grads = [[0.0, 0.0] for layer in range(layers)]
    kept = {}
    for turn in range(STEPS):
        cot = of_turn(cots, turn).astype(F32)
        if turn == 0:
            adjoint = cot
        elif turn == 2:
            adjoint = cot + over_step(adjoint.astype(BF16), 3).astype(F32)
        else:
            adjoint = adjoint + cot
        for layer in range(layers - 1, -1, -1):
            wa, wb, wc = w[layer]
            ab = adjoint.astype(BF16)
            dzb = (mul_t(ab, wc) * of_turn(slopes[layer], turn).astype(F32)).astype(BF16)
            dm = mul_t(dzb, wb).astype(BF16)
            kept[turn, layer] = (ab, dzb)
            if turn == 1 and layer == 0:
                dm, other = lax.optimization_barrier((dm, lhs[1]))
                lhs = (lhs[0], other)
            d_out = over_node(dm, OUTER)
            adjoint = adjoint + mul_t(dzb, wa) + t_mul(m_own, dm)
            d_sib = over_node(after(dm, adjoint), SIBLING)
            if turn == 0 and layer == layers - 1:
                ordered = [mul(v, choice).astype(BF16) for v in after(tuple(left_hand), dm)]
                parts = [
                    jnp.concatenate([v[:, k * share : (k + 1) * share] for v in ordered], axis=1)
                    for k in range(SPLIT)
                ]
            if turn == 0 and layer == 0:
                lhs = (parts[0], over_step(after(parts[1], dm), 1))
            if turn >= 2:
                early = kept[turn - 2, layer]
                late = (ab, dzb) if turn == STEPS - 1 and layer == 0 else after((ab, dzb), dm)
                pair = [jnp.where(upper, e, v) for e, v in zip(early, late)]
                grads[layer] = add_grads(grads[layer], of_turn(lhs, turn), pair, layer)
            if turn == STEPS - 1:
                grads[layer] = core_sum(grads[layer])
            adjoint = adjoint + t_mul(n_sib, d_sib) + t_mul(n_out, d_out)
        result = jnp.where(x == STEPS - 1 - turn, adjoint, result)
    result = over_node(result.astype(BF16), FLIP).astype(F32)

    mats = 3 * layers
    grad = jnp.concatenate(grads, axis=0).reshape(mats, Y, -1, width)
    grad_b = grad.astype(BF16)
    total = grad[:, 0]
    for k in (2, 1, 3):
        sent = grad_b[:, k].reshape(-1, width)
        total = total + over_node(sent, y_pairs(k)).astype(F32).reshape(total.shape)
    sent = total.astype(BF16).reshape(mats, Z, -1, width).transpose(1, 0, 2, 3)
    got = lax.all_to_all(sent.reshape(Z, -1, width), "node", 0, 0, axis_index_groups=Z_GROUPS, tiled=False)
    mine = jnp.sum(got.astype(F32), axis=0).astype(BF16)
    beside, same, across = [over_step(mine, k).astype(F32) for k in (1, 2, 3)]
    mine, beside = mine.astype(F32) + same, beside + across
    low = jnp.where(own_first, beside, mine)
    high = jnp.where(own_first, mine, beside)
    scale = 1.0 / math.sqrt(STEPS * rows * NODES)
    gradient = jnp.stack([low, high], axis=0) * scale
    gradient = gradient.reshape(SPLIT, mats, -1, width).transpose(0, 2, 1, 3)
    return (result[None], gradient.reshape(-1, mats * width))


def add_grads(sums, lhs, pair, layer):
    share = lhs.shape[1] // 6
    ab, dzb = pair
    base = 3 * layer * share
    both = t_mul(lhs[:, base : base + 2 * share], dzb)
    last = t_mul(lhs[:, base + 2 * share : base + 3 * share], ab)
    return [sums[0] + both, sums[1] + last]


def core_sum(sums):
    both, last = sums
    share = last.shape[0]
    half = share // C
    parts = [both[:share], both[share:], last]
    sent = jnp.concatenate([v[half:] for v in parts], axis=0).astype(BF16)
    return jnp.concatenate([v[:half] for v in parts], axis=0) + over_node(sent, SIBLING).astype(F32)


def solution(mesh):
    return jax.shard_map(
        on_device,
        mesh=mesh,
        in_specs=(
            P("step", "node", None),
            P("step", "node", None),
            P(),
            P("node", None, None, None),
            P("node", None),
            P("node", None),
            P("node"),
        ),
        out_specs=(P("step", "node", None), P("node", None)),
        check_vma=False,
    )
```

```python
import math

import jax
import jax.numpy as jnp
from jax import lax
from jax.sharding import PartitionSpec as P

Z, Y, C = 8, 4, 2
NODES = Z * Y * C
STEPS = 4
SPLIT = 2
F32 = jnp.float32
BF16 = jnp.bfloat16


def place(z, y, c):
    return (z * Y + y) * C + c


def split(p):
    return p // (Y * C), (p // C) % Y, p % C


def snake(p):
    z, y, c = split(p)
    return place(z, y if z % 2 == 0 else Y - 1 - y, c)


def beyond(q):
    return (q + 1) % NODES if q % 2 else (q - 1) % NODES


DEVICES = range(NODES)
FLIP = [(snake(p), p) for p in DEVICES]
OUTER = [(p, snake(beyond(snake(p)))) for p in DEVICES]
SIBLING = [(p, p ^ 1) for p in DEVICES]
Z_GROUPS = [[place(z, y, c) for z in range(Z)] for y in range(Y) for c in range(C)]


def over_node(value, pairs):
    return lax.ppermute(value, "node", pairs)


def over_step(value, k):
    return lax.ppermute(value, "step", [(s, s ^ k) for s in range(STEPS)])


def over_both(value, k):
    pairs = [((s ^ k) * NODES + snake(p), s * NODES + p) for s in range(STEPS) for p in DEVICES]
    return lax.ppermute(value, ("step", "node"), pairs)


def y_pairs(k):
    return [(place(z, y, c), place(z, y ^ k, c)) for z in range(Z) for y in range(Y) for c in range(C)]


def mul(left, right):
    return jnp.dot(left, right, preferred_element_type=F32)


def mul_t(left, right):
    return lax.dot_general(left, right, (((1,), (1,)), ((), ())), preferred_element_type=F32)


def t_mul(left, right):
    return lax.dot_general(left, right, (((0,), (0,)), ((), ())), preferred_element_type=F32)


def assemble(tiles, sources, targets, count, core, nblk):
    slots, block = tiles.shape[0], tiles.shape[1]
    third = sources // nblk
    third = jnp.where(core == 1, 2 - third, third)
    column = third * nblk + sources % nblk
    cell = targets * (3 * nblk) + column
    live = jnp.arange(slots) < count
    hot = ((cell[None, :] == jnp.arange(3 * nblk * nblk)[:, None]) & live[None, :]).astype(BF16)
    blocks = lax.dot_general(hot, tiles, (((1,), (0,)), ((), ())), preferred_element_type=F32)
    blocks = blocks.astype(BF16).reshape(nblk, 3 * nblk, block, block)
    return blocks.transpose(0, 2, 1, 3).reshape(nblk * block, 3 * nblk * block)


def feature_choice(width, x, yi, ci, per):
    column = lax.broadcasted_iota(jnp.int32, (width, width), 1)
    row = lax.broadcasted_iota(jnp.int32, (width, width), 0)
    row_of = column % per
    rest = column // per
    z, rest = rest % Z, rest // Z
    y, rest = rest % Y, rest // Y
    c, k = rest % C, rest // C
    feature = place(z, y ^ yi, c ^ ci) * (per * SPLIT) + ((x & 1) ^ k) * per + row_of
    return (row == feature).astype(BF16)


def after(value, *others):
    return lax.optimization_barrier((value, *others))[0]


def on_device(states, step_cotangents, weights, edge_tiles, tile_src, tile_dst, tile_counts):
    rows, width = states.shape[1], states.shape[2]
    layers = weights.shape[1] // (3 * width)
    nblk = rows // edge_tiles.shape[2]
    me = lax.axis_index("node")
    x = lax.axis_index("step")
    zi, yi, ci = split(me)
    w = [
        [weights[:, (3 * layer + j) * width : (3 * layer + j + 1) * width] for j in range(3)]
        for layer in range(layers)
    ]

    hb = over_node(states[0], FLIP)
    outer = over_node(hb, OUTER)
    matrix = assemble(edge_tiles[0], tile_src[0], tile_dst[0], tile_counts[0], ci, nblk)
    cot = after(step_cotangents[0], matrix).astype(BF16)
    matrix = over_node(matrix, FLIP)
    m_out, m_own, m_sib = (matrix[:, j * rows : (j + 1) * rows] for j in range(3))
    cots = (over_node(cot, FLIP), over_node(over_step(cot, 1), FLIP))

    h = hb.astype(F32)
    left_hand, slopes = [], []
    for layer in range(layers):
        wa, wb, wc = w[layer]
        if layer:
            hb = h.astype(BF16)
            outer = over_node(hb, OUTER)
        sib = over_node(hb, SIBLING)
        local = mul(m_own, hb)
        first = mul(hb, wa)
        mb = (local + mul(m_sib, sib) + mul(m_out, outer)).astype(BF16)
        zz = first + mul(mb, wb)
        sig = jax.nn.sigmoid(zz)
        g = (zz * sig).astype(BF16)
        slope = (sig * (1.0 + zz * (1.0 - sig))).astype(BF16)
        if layer + 1 < layers:
            h = h + mul(g, wc)
        slopes.append([slope, over_step(slope, 1) if layer else None])
        left_hand += [hb, mb, g]
    n_out = over_node(m_out, OUTER)
    n_sib = over_node(m_sib, SIBLING)

    own_first = (x & 1) == 1

    def of_turn(pair, turn):
        own, other = pair
        return jnp.where(own_first, other, own) if turn % 2 else jnp.where(own_first, own, other)

    upper = x >= 2
    share = width // SPLIT
    choice = feature_choice(width, x, yi, ci, width // NODES // SPLIT)
    crossing = {(0, 0): 1, (1, 0): 0}
    arrived = {(1, 0): 1, (2, 1): 0}

    def add_rows(grads, lhs, kept, turn, layer):
        both, last = grads[layer]
        pair = [jnp.where(upper, e, v) for e, v in zip(kept[turn - 2, layer], kept[turn, layer])]
        left = of_turn(lhs[layer], turn)
        both = both + t_mul(left[:, : 2 * share], pair[1])
        return both, last + t_mul(left[:, 2 * share :], pair[0])

    adjoint = None
    result = jnp.zeros((rows, width), F32)
    grads = [(0.0, 0.0) for layer in range(layers)]
    kept = {}
    for turn in range(STEPS):
        cot = of_turn(cots, turn).astype(F32)
        if turn == 0:
            adjoint = cot
        elif turn == 2:
            adjoint = cot + over_step(adjoint.astype(BF16), 3).astype(F32)
        else:
            adjoint = adjoint + cot
        for layer in range(layers - 1, -1, -1):
            wa, wb, wc = w[layer]
            ab = adjoint.astype(BF16)
            dzb = (mul_t(ab, wc) * of_turn(slopes[layer], turn).astype(F32)).astype(BF16)
            dm = mul_t(dzb, wb).astype(BF16)
            kept[turn, layer] = (ab, dzb)
            if (turn, layer) in arrived:
                k = arrived[turn, layer]
                dm, lhs[k][1] = lax.optimization_barrier((dm, lhs[k][1]))
            if turn == STEPS - 1 and layer == 0:
                sums = add_rows(grads, lhs, kept, turn, layer)
                keep, sent = split_cores(sums)
                grads[0] = keep + over_node(sent, SIBLING).astype(F32)
                dm = after(dm, sent)
            d_out = over_node(dm, OUTER)
            adjoint = adjoint + mul_t(dzb, wa) + t_mul(m_own, dm)
            d_sib = over_node(after(dm, adjoint), SIBLING)
            if turn == 0 and layer == layers - 1:
                slopes[0][1] = over_step(after(slopes[0][0], dm), 1)
                ordered = [mul(v, choice).astype(BF16) for v in after(tuple(left_hand), dm)]
                parts = []
                for k in range(layers):
                    three = ordered[3 * k : 3 * k + 3]
                    parts.append([
                        jnp.concatenate([v[:, j * share : (j + 1) * share] for v in three], axis=1)
                        for j in range(SPLIT)
                    ])
                lhs = [[p[0], None] for p in parts]
            if (turn, layer) in crossing:
                k = crossing[turn, layer]
                lhs[k][1] = over_step(after(parts[k][1], dm), 1)
            if turn >= 2 and (turn, layer) != (STEPS - 1, 0):
                kept[turn, layer] = after((ab, dzb), dm)
                grads[layer] = add_rows(grads, lhs, kept, turn, layer)
                if turn == STEPS - 1:
                    keep, sent = split_cores(grads[layer])
                    grads[layer] = keep + over_node(sent, SIBLING).astype(F32)
            adjoint = adjoint + t_mul(n_sib, d_sib) + t_mul(n_out, d_out)
        result = jnp.where(x == STEPS - 1 - turn, adjoint, result)
    result = over_node(result.astype(BF16), FLIP).astype(F32)

    grad = jnp.concatenate(grads, axis=1)
    grad_b = grad.astype(BF16)
    chunk = grad.shape[0] // Y
    total = grad[:chunk]
    for k in (2, 1, 3):
        total = total + over_node(grad_b[k * chunk : (k + 1) * chunk], y_pairs(k)).astype(F32)
    sent = total.astype(BF16).reshape(Z, chunk // Z, -1)
    got = lax.all_to_all(sent, "node", 0, 0, axis_index_groups=Z_GROUPS, tiled=False)
    mine = jnp.sum(got.astype(F32), axis=0).astype(BF16)
    beside, same, across = [over_step(mine, k).astype(F32) for k in (1, 2, 3)]
    mine, beside = mine.astype(F32) + same, beside + across
    low = jnp.where(own_first, beside, mine)
    high = jnp.where(own_first, mine, beside)
    scale = 1.0 / math.sqrt(STEPS * rows * NODES)
    return (result[None], jnp.concatenate([low, high], axis=0) * scale)


def split_cores(sums):
    both, last = sums
    share = last.shape[0]
    half = share // C
    parts = [both[:share], both[share:], last]
    keep = jnp.concatenate([v[:half] for v in parts], axis=1)
    return keep, jnp.concatenate([v[half:] for v in parts], axis=1).astype(BF16)


def solution(mesh):
    return jax.shard_map(
        on_device,
        mesh=mesh,
        in_specs=(
            P("step", "node", None),
            P("step", "node", None),
            P(),
            P("node", None, None, None),
            P("node", None),
            P("node", None),
            P("node"),
        ),
        out_specs=(P("step", "node", None), P("node", None)),
        check_vma=False,
    )
```

```python
import math

import jax
import jax.numpy as jnp
from jax import lax
from jax.sharding import PartitionSpec as P

Z, Y, C = 8, 4, 2
NODES = Z * Y * C
STEPS = 4
SPLIT = 2
F32 = jnp.float32
BF16 = jnp.bfloat16


def place(z, y, c):
    return (z * Y + y) * C + c


def split(p):
    return p // (Y * C), (p // C) % Y, p % C


def snake(p):
    z, y, c = split(p)
    return place(z, y if z % 2 == 0 else Y - 1 - y, c)


def beyond(q):
    return (q + 1) % NODES if q % 2 else (q - 1) % NODES


DEVICES = range(NODES)
FLIP = [(snake(p), p) for p in DEVICES]
OUTER = [(p, snake(beyond(snake(p)))) for p in DEVICES]
OUTER_HOME = [(beyond(snake(p)), p) for p in DEVICES]
SIBLING = [(p, p ^ 1) for p in DEVICES]
Z_GROUPS = [[place(z, y, c) for z in range(Z)] for y in range(Y) for c in range(C)]


def over_node(value, pairs):
    return lax.ppermute(value, "node", pairs)


def over_step(value, k):
    return lax.ppermute(value, "step", [(s, s ^ k) for s in range(STEPS)])


def over_both(value, k):
    pairs = [((s ^ k) * NODES + snake(p), s * NODES + p) for s in range(STEPS) for p in DEVICES]
    return lax.ppermute(value, ("step", "node"), pairs)


def y_pairs(k):
    return [(place(z, y, c), place(z, y ^ k, c)) for z in range(Z) for y in range(Y) for c in range(C)]


def mul(left, right):
    return jnp.dot(left, right, preferred_element_type=F32)


def mul_t(left, right):
    return lax.dot_general(left, right, (((1,), (1,)), ((), ())), preferred_element_type=F32)


def t_mul(left, right):
    return lax.dot_general(left, right, (((0,), (0,)), ((), ())), preferred_element_type=F32)


def assemble(tiles, sources, targets, count, core, nblk):
    slots, block = tiles.shape[0], tiles.shape[1]
    third = sources // nblk
    third = jnp.where(core == 1, 2 - third, third)
    column = third * nblk + sources % nblk
    cell = targets * (3 * nblk) + column
    live = jnp.arange(slots) < count
    hot = ((cell[None, :] == jnp.arange(3 * nblk * nblk)[:, None]) & live[None, :]).astype(BF16)
    blocks = lax.dot_general(hot, tiles, (((1,), (0,)), ((), ())), preferred_element_type=F32)
    blocks = blocks.astype(BF16).reshape(nblk, 3 * nblk, block, block)
    return blocks.transpose(0, 2, 1, 3).reshape(nblk * block, 3 * nblk * block)


def feature_choice(width, x, yi, ci, per):
    column = lax.broadcasted_iota(jnp.int32, (width, width), 1)
    row = lax.broadcasted_iota(jnp.int32, (width, width), 0)
    row_of = column % per
    rest = column // per
    z, rest = rest % Z, rest // Z
    y, rest = rest % Y, rest // Y
    c, k = rest % C, rest // C
    feature = place(z, y ^ yi, c ^ ci) * (per * SPLIT) + ((x & 1) ^ k) * per + row_of
    return (row == feature).astype(BF16)


def after(value, *others):
    return lax.optimization_barrier((value, *others))[0]


def on_device(states, step_cotangents, weights, edge_tiles, tile_src, tile_dst, tile_counts):
    rows, width = states.shape[1], states.shape[2]
    layers = weights.shape[1] // (3 * width)
    nblk = rows // edge_tiles.shape[2]
    me = lax.axis_index("node")
    x = lax.axis_index("step")
    zi, yi, ci = split(me)
    w = [
        [weights[:, (3 * layer + j) * width : (3 * layer + j + 1) * width] for j in range(3)]
        for layer in range(layers)
    ]

    hb = over_node(states[0], FLIP)
    outer = over_node(states[0], OUTER_HOME)
    matrix = assemble(edge_tiles[0], tile_src[0], tile_dst[0], tile_counts[0], ci, nblk)
    cot = after(step_cotangents[0], matrix).astype(BF16)
    matrix = over_node(matrix, FLIP)
    m_out, m_own, m_sib = (matrix[:, j * rows : (j + 1) * rows] for j in range(3))
    cot = over_node(cot, FLIP)

    h = hb.astype(F32)
    left_hand, slopes = [], []
    for layer in range(layers):
        wa, wb, wc = w[layer]
        if layer:
            hb = h.astype(BF16)
            outer = over_node(hb, OUTER)
        sib = over_node(hb, SIBLING)
        local = mul(m_own, hb)
        first = mul(hb, wa)
        mb = (local + mul(m_sib, sib) + mul(m_out, outer)).astype(BF16)
        zz = first + mul(mb, wb)
        sig = jax.nn.sigmoid(zz)
        g = (zz * sig).astype(BF16)
        slope = (sig * (1.0 + zz * (1.0 - sig))).astype(BF16)
        if layer + 1 < layers:
            h = h + mul(g, wc)
            slope = after(slope, h)
        slopes.append((slope, over_step(slope, 1)))
        left_hand += [hb, mb, g]
    cot = after(cot, left_hand[3])
    cots = (cot, over_step(cot, 1))
    n_out = over_node(m_out, OUTER)
    n_sib = over_node(m_sib, SIBLING)

    own_first = (x & 1) == 1

    def of_turn(pair, turn):
        own, other = pair
        return jnp.where(own_first, other, own) if turn % 2 else jnp.where(own_first, own, other)

    upper = x >= 2
    share = width // SPLIT
    choice = feature_choice(width, x, yi, ci, width // NODES // SPLIT)
    crossing = {(0, 0): [3], (1, 1): [4], (1, 0): [5, 0], (2, 1): [1], (2, 0): [2]}

    def add_rows(grads, lhs, kept, turn, layer):
        both, last = grads[layer]
        pair = [jnp.where(upper, e, v) for e, v in zip(kept[turn - 2, layer], kept[turn, layer])]
        left = [of_turn(v, turn) for v in lhs[3 * layer : 3 * layer + 3]]
        both = both + t_mul(jnp.concatenate(left[:2], axis=1), pair[1])
        return both, last + t_mul(left[2], pair[0])

    adjoint = None
    result = jnp.zeros((rows, width), F32)
    grads = [(0.0, 0.0) for layer in range(layers)]
    kept, moving = {}, []
    for turn in range(STEPS):
        cot = of_turn(cots, turn).astype(F32)
        if turn == 0:
            adjoint = cot
        elif turn == 2:
            adjoint = cot + over_step(adjoint.astype(BF16), 3).astype(F32)
        else:
            adjoint = adjoint + cot
        for layer in range(layers - 1, -1, -1):
            wa, wb, wc = w[layer]
            ab = adjoint.astype(BF16)
            dzb = (mul_t(ab, wc) * of_turn(slopes[layer], turn).astype(F32)).astype(BF16)
            dm = mul_t(dzb, wb).astype(BF16)
            kept[turn, layer] = (ab, dzb)
            if moving:
                dm, got = lax.optimization_barrier((dm, tuple(lhs[k][1] for k in moving)))
                for k, v in zip(moving, got):
                    lhs[k][1] = v
                moving = []
            if turn == STEPS - 1 and layer == 0:
                sums = add_rows(grads, lhs, kept, turn, layer)
                keep, sent = split_cores(sums)
                grads[0] = keep + over_node(sent, SIBLING).astype(F32)
                dm = after(dm, sent)
            d_out = over_node(dm, OUTER)
            adjoint = adjoint + mul_t(dzb, wa) + t_mul(m_own, dm)
            d_sib = over_node(after(dm, adjoint), SIBLING)
            if turn == 0 and layer == layers - 1:
                ordered = [mul(v, choice).astype(BF16) for v in after(tuple(left_hand), dm)]
                lhs = [[v[:, :share], v[:, share:]] for v in ordered]
            if (turn, layer) in crossing:
                moving = crossing[turn, layer]
                joined = jnp.concatenate([after(lhs[k][1], dm) for k in moving], axis=1)
                joined = over_step(joined, 1)
                for j, k in enumerate(moving):
                    lhs[k][1] = joined[:, j * share : (j + 1) * share]
            if turn >= 2 and (turn, layer) != (STEPS - 1, 0):
                kept[turn, layer] = after((ab, dzb), dm)
                if layer == 1:
                    grads[layer] = add_rows(grads, lhs, kept, turn, layer)
                if turn == STEPS - 1:
                    grads[0] = add_rows(grads, lhs, kept, 2, 0)
                    keep, sent = split_cores(grads[layer])
                    grads[layer] = keep + over_node(sent, SIBLING).astype(F32)
            adjoint = adjoint + t_mul(n_sib, d_sib) + t_mul(n_out, d_out)
        result = jnp.where(x == STEPS - 1 - turn, adjoint, result)
    result = over_node(result.astype(BF16), FLIP).astype(F32)

    grad = jnp.concatenate(grads, axis=1)
    grad_b = grad.astype(BF16)
    chunk = grad.shape[0] // Y
    total = grad[:chunk]
    for k in (2, 1, 3):
        total = total + over_node(grad_b[k * chunk : (k + 1) * chunk], y_pairs(k)).astype(F32)
    sent = total.astype(BF16).reshape(Z, chunk // Z, -1)
    got = lax.all_to_all(sent, "node", 0, 0, axis_index_groups=Z_GROUPS, tiled=False)
    mine = jnp.sum(got.astype(F32), axis=0).astype(BF16)
    beside, same, across = [over_step(mine, k).astype(F32) for k in (1, 2, 3)]
    mine, beside = mine.astype(F32) + same, beside + across
    low = jnp.where(own_first, beside, mine)
    high = jnp.where(own_first, mine, beside)
    scale = 1.0 / math.sqrt(STEPS * rows * NODES)
    return (result[None], jnp.concatenate([low, high], axis=0) * scale)


def split_cores(sums):
    both, last = sums
    share = last.shape[0]
    half = share // C
    parts = [both[:share], both[share:], last]
    keep = jnp.concatenate([v[:half] for v in parts], axis=1)
    return keep, jnp.concatenate([v[half:] for v in parts], axis=1).astype(BF16)


def solution(mesh):
    return jax.shard_map(
        on_device,
        mesh=mesh,
        in_specs=(
            P("step", "node", None),
            P("step", "node", None),
            P(),
            P("node", None, None, None),
            P("node", None),
            P("node", None),
            P("node"),
        ),
        out_specs=(P("step", "node", None), P("node", None)),
        check_vma=False,
    )
```

```python
import math

import jax
import jax.numpy as jnp
from jax import lax
from jax.sharding import PartitionSpec as P

Z, Y, C = 8, 4, 2
NODES = Z * Y * C
STEPS = 4
SPLIT = 2
F32 = jnp.float32
BF16 = jnp.bfloat16


def place(z, y, c):
    return (z * Y + y) * C + c


def split(p):
    return p // (Y * C), (p // C) % Y, p % C


def snake(p):
    z, y, c = split(p)
    return place(z, y if z % 2 == 0 else Y - 1 - y, c)


def beyond(q):
    return (q + 1) % NODES if q % 2 else (q - 1) % NODES


DEVICES = range(NODES)
FLIP = [(snake(p), p) for p in DEVICES]
OUTER = [(p, snake(beyond(snake(p)))) for p in DEVICES]
OUTER_HOME = [(beyond(snake(p)), p) for p in DEVICES]
SIBLING = [(p, p ^ 1) for p in DEVICES]
Z_GROUPS = [[place(z, y, c) for z in range(Z)] for y in range(Y) for c in range(C)]


def over_node(value, pairs):
    return lax.ppermute(value, "node", pairs)


def over_step(value, k):
    return lax.ppermute(value, "step", [(s, s ^ k) for s in range(STEPS)])


def over_both(value, k):
    pairs = [((s ^ k) * NODES + snake(p), s * NODES + p) for s in range(STEPS) for p in DEVICES]
    return lax.ppermute(value, ("step", "node"), pairs)


def y_pairs(k):
    return [(place(z, y, c), place(z, y ^ k, c)) for z in range(Z) for y in range(Y) for c in range(C)]


def mul(left, right):
    return jnp.dot(left, right, preferred_element_type=F32)


def mul_t(left, right):
    return lax.dot_general(left, right, (((1,), (1,)), ((), ())), preferred_element_type=F32)


def t_mul(left, right):
    return lax.dot_general(left, right, (((0,), (0,)), ((), ())), preferred_element_type=F32)


def assemble(tiles, sources, targets, count, core, nblk):
    slots, block = tiles.shape[0], tiles.shape[1]
    third = sources // nblk
    third = jnp.where(core == 1, 2 - third, third)
    column = third * nblk + sources % nblk
    cell = targets * (3 * nblk) + column
    live = jnp.arange(slots) < count
    hot = ((cell[None, :] == jnp.arange(3 * nblk * nblk)[:, None]) & live[None, :]).astype(BF16)
    blocks = lax.dot_general(hot, tiles, (((1,), (0,)), ((), ())), preferred_element_type=F32)
    blocks = blocks.astype(BF16).reshape(nblk, 3 * nblk, block, block)
    return blocks.transpose(0, 2, 1, 3).reshape(nblk * block, 3 * nblk * block)


def feature_choice(width, x, yi, ci, per):
    column = lax.broadcasted_iota(jnp.int32, (1, width), 1)
    row = lax.broadcasted_iota(jnp.int32, (width, 1), 0)
    row_of = column % per
    rest = column // per
    z, rest = rest % Z, rest // Z
    y, rest = rest % Y, rest // Y
    c, k = rest % C, rest // C
    feature = place(z, y ^ yi, c ^ ci) * (per * SPLIT) + ((x & 1) ^ k) * per + row_of
    return (row == feature).astype(BF16)


def after(value, *others):
    return lax.optimization_barrier((value, *others))[0]


def on_device(states, step_cotangents, weights, edge_tiles, tile_src, tile_dst, tile_counts):
    rows, width = states.shape[1], states.shape[2]
    layers = weights.shape[1] // (3 * width)
    nblk = rows // edge_tiles.shape[2]
    me = lax.axis_index("node")
    x = lax.axis_index("step")
    zi, yi, ci = split(me)
    w = [
        [weights[:, (3 * layer + j) * width : (3 * layer + j + 1) * width] for j in range(3)]
        for layer in range(layers)
    ]

    hb = over_node(states[0], FLIP)
    outer = over_node(states[0], OUTER_HOME)
    matrix = assemble(edge_tiles[0], tile_src[0], tile_dst[0], tile_counts[0], ci, nblk)
    cot = after(step_cotangents[0], matrix).astype(BF16)
    matrix = over_node(matrix, FLIP)
    m_out, m_own, m_sib = (matrix[:, j * rows : (j + 1) * rows] for j in range(3))
    cot = over_node(cot, FLIP)

    h = hb.astype(F32)
    left_hand, slopes = [], []
    for layer in range(layers):
        wa, wb, wc = w[layer]
        if layer:
            hb = h.astype(BF16)
            outer = over_node(hb, OUTER)
        sib = over_node(hb, SIBLING)
        local = mul(m_own, hb)
        first = mul(hb, wa)
        mb = (local + mul(m_sib, sib) + mul(m_out, outer)).astype(BF16)
        zz = first + mul(mb, wb)
        sig = jax.nn.sigmoid(zz)
        g = (zz * sig).astype(BF16)
        slope = (sig * (1.0 + zz * (1.0 - sig))).astype(BF16)
        if layer + 1 < layers:
            h = h + mul(g, wc)
            slope = after(slope, h)
        slopes.append((slope, over_step(slope, 1)))
        left_hand += [hb, mb, g]
    cot = after(cot, left_hand[3])
    cots = (cot, over_step(cot, 1))
    n_out = over_node(m_out, OUTER)
    n_chip = jnp.concatenate([m_own, over_node(m_sib, SIBLING)], axis=0)

    own_first = (x & 1) == 1

    def of_turn(pair, turn):
        own, other = pair
        return jnp.where(own_first, other, own) if turn % 2 else jnp.where(own_first, own, other)

    upper = x >= 2
    share = width // SPLIT
    choice = feature_choice(width, x, yi, ci, width // NODES // SPLIT)
    crossing = {(1, 0): [3, 4, 5, 0], (2, 0): [1, 2]}

    def sum_rows(layer):
        pairs = [
            [jnp.where(upper, e, v) for e, v in zip(kept[turn - 2, layer], kept[turn, layer])]
            for turn in (2, 3)
        ]
        ab, dzb = [jnp.concatenate(v, axis=0) for v in zip(*pairs)]
        left = [
            jnp.concatenate([of_turn(v, turn) for turn in (2, 3)], axis=0)
            for v in lhs[3 * layer : 3 * layer + 3]
        ]
        return t_mul(jnp.concatenate(left[:2], axis=1), dzb), t_mul(left[2], ab)

    adjoint = None
    result = jnp.zeros((rows, width), F32)
    grads = [None] * layers
    kept, moving = {}, []
    for turn in range(STEPS):
        cot = of_turn(cots, turn).astype(F32)
        if turn == 0:
            adjoint = cot
        elif turn == 2:
            adjoint = cot + over_step(adjoint.astype(BF16), 3).astype(F32)
        else:
            adjoint = adjoint + cot
        for layer in range(layers - 1, -1, -1):
            wa, wb, wc = w[layer]
            ab = adjoint.astype(BF16)
            dzb = (mul_t(ab, wc) * of_turn(slopes[layer], turn).astype(F32)).astype(BF16)
            dm = mul_t(dzb, wb).astype(BF16)
            kept[turn, layer] = (ab, dzb)
            if moving:
                dm, got = lax.optimization_barrier((dm, tuple(lhs[k][1] for k in moving)))
                for k, v in zip(moving, got):
                    lhs[k][1] = v
                moving = []
            if turn == STEPS - 1 and layer == 0:
                keep, sent = split_cores(sum_rows(layer))
                grads[0] = keep + over_node(sent, SIBLING).astype(F32)
                dm = after(dm, sent)
            d_out = over_node(dm, OUTER)
            adjoint = adjoint + mul_t(dzb, wa)
            d_sib = over_node(after(dm, adjoint), SIBLING)
            if turn == 0 and layer == layers - 1:
                ordered = mul(jnp.concatenate(after(tuple(left_hand), dm), axis=0), choice).astype(BF16)
                ordered = ordered.reshape(len(left_hand), rows, width)
                lhs = [[v[:, :share], v[:, share:]] for v in ordered]
            if (turn, layer) in crossing:
                moving = crossing[turn, layer]
                joined = jnp.concatenate([after(lhs[k][1], dm) for k in moving], axis=1)
                joined = over_step(joined, 1)
                for j, k in enumerate(moving):
                    lhs[k][1] = joined[:, j * share : (j + 1) * share]
            if turn == STEPS - 1 and layer:
                kept[turn, layer] = after((ab, dzb), dm)
                keep, sent = split_cores(sum_rows(layer))
                grads[layer] = keep + over_node(sent, SIBLING).astype(F32)
            adjoint = adjoint + t_mul(n_chip, jnp.concatenate([dm, d_sib], axis=0)) + t_mul(n_out, d_out)
        result = jnp.where(x == STEPS - 1 - turn, adjoint, result)
    result = over_node(result.astype(BF16), FLIP).astype(F32)

    grad = jnp.concatenate(grads, axis=1)
    grad_b = grad.astype(BF16)
    chunk = grad.shape[0] // Y
    total = grad[:chunk]
    for k in (2, 1, 3):
        total = total + over_node(grad_b[k * chunk : (k + 1) * chunk], y_pairs(k)).astype(F32)
    sent = total.astype(BF16).reshape(Z, chunk // Z, -1)
    got = lax.all_to_all(sent, "node", 0, 0, axis_index_groups=Z_GROUPS, tiled=False)
    mine = jnp.sum(got.astype(F32), axis=0).astype(BF16)
    beside, same, across = [over_step(mine, k).astype(F32) for k in (1, 2, 3)]
    mine, beside = mine.astype(F32) + same, beside + across
    low = jnp.where(own_first, beside, mine)
    high = jnp.where(own_first, mine, beside)
    scale = 1.0 / math.sqrt(STEPS * rows * NODES)
    return (result[None], jnp.concatenate([low, high], axis=0) * scale)


def split_cores(sums):
    both, last = sums
    share = last.shape[0]
    half = share // C
    parts = [both[:share], both[share:], last]
    keep = jnp.concatenate([v[:half] for v in parts], axis=1)
    return keep, jnp.concatenate([v[half:] for v in parts], axis=1).astype(BF16)


def solution(mesh):
    return jax.shard_map(
        on_device,
        mesh=mesh,
        in_specs=(
            P("step", "node", None),
            P("step", "node", None),
            P(),
            P("node", None, None, None),
            P("node", None),
            P("node", None),
            P("node"),
        ),
        out_specs=(P("step", "node", None), P("node", None)),
        check_vma=False,
    )
```

```python
import math

import jax
import jax.numpy as jnp
from jax import lax
from jax.sharding import PartitionSpec as P

Z, Y, C = 8, 4, 2
NODES = Z * Y * C
STEPS = 4
SPLIT = 2
F32 = jnp.float32
BF16 = jnp.bfloat16


def place(z, y, c):
    return (z * Y + y) * C + c


def split(p):
    return p // (Y * C), (p // C) % Y, p % C


def snake(p):
    z, y, c = split(p)
    return place(z, y if z % 2 == 0 else Y - 1 - y, c)


def beyond(q):
    return (q + 1) % NODES if q % 2 else (q - 1) % NODES


DEVICES = range(NODES)
FLIP = [(snake(p), p) for p in DEVICES]
OUTER = [(p, snake(beyond(snake(p)))) for p in DEVICES]
OUTER_HOME = [(beyond(snake(p)), p) for p in DEVICES]
SIBLING = [(p, p ^ 1) for p in DEVICES]
Z_GROUPS = [[place(z, y, c) for z in range(Z)] for y in range(Y) for c in range(C)]


def over_node(value, pairs):
    return lax.ppermute(value, "node", pairs)


def over_step(value, k):
    return lax.ppermute(value, "step", [(s, s ^ k) for s in range(STEPS)])


def over_both(value, k):
    pairs = [((s ^ k) * NODES + snake(p), s * NODES + p) for s in range(STEPS) for p in DEVICES]
    return lax.ppermute(value, ("step", "node"), pairs)


def y_pairs(k):
    return [(place(z, y, c), place(z, y ^ k, c)) for z in range(Z) for y in range(Y) for c in range(C)]


def mul(left, right):
    return jnp.dot(left, right, preferred_element_type=F32)


def mul_t(left, right):
    return lax.dot_general(left, right, (((1,), (1,)), ((), ())), preferred_element_type=F32)


def t_mul(left, right):
    return lax.dot_general(left, right, (((0,), (0,)), ((), ())), preferred_element_type=F32)


def assemble(tiles, sources, targets, count, core, nblk):
    slots, block = tiles.shape[0], tiles.shape[1]
    third = sources // nblk
    third = jnp.where(core == 1, 2 - third, third)
    column = third * nblk + sources % nblk
    cell = targets * (3 * nblk) + column
    live = jnp.arange(slots) < count
    hot = ((cell[None, :] == jnp.arange(3 * nblk * nblk)[:, None]) & live[None, :]).astype(BF16)
    blocks = lax.dot_general(hot, tiles, (((1,), (0,)), ((), ())), preferred_element_type=F32)
    blocks = blocks.astype(BF16).reshape(nblk, 3 * nblk, block, block)
    return blocks.transpose(0, 2, 1, 3).reshape(nblk * block, 3 * nblk * block)


def feature_choice(width, x, yi, ci, per):
    column = lax.broadcasted_iota(jnp.int32, (1, width), 1)
    row = lax.broadcasted_iota(jnp.int32, (width, 1), 0)
    row_of = column % per
    rest = column // per
    z, rest = rest % Z, rest // Z
    y, rest = rest % Y, rest // Y
    c, k = rest % C, rest // C
    feature = place(z, y ^ yi, c ^ ci) * (per * SPLIT) + ((x & 1) ^ k) * per + row_of
    return (row == feature).astype(BF16)


def after(value, *others):
    return lax.optimization_barrier((value, *others))[0]


def on_device(states, step_cotangents, weights, edge_tiles, tile_src, tile_dst, tile_counts):
    rows, width = states.shape[1], states.shape[2]
    layers = weights.shape[1] // (3 * width)
    nblk = rows // edge_tiles.shape[2]
    me = lax.axis_index("node")
    x = lax.axis_index("step")
    zi, yi, ci = split(me)
    w = [
        [weights[:, (3 * layer + j) * width : (3 * layer + j + 1) * width] for j in range(3)]
        for layer in range(layers)
    ]

    hb = over_node(states[0], FLIP)
    outer = over_node(states[0], OUTER_HOME)
    matrix = assemble(edge_tiles[0], tile_src[0], tile_dst[0], tile_counts[0], ci, nblk)
    cot = after(step_cotangents[0], matrix).astype(BF16)
    matrix = over_node(matrix, FLIP)
    m_out, m_own, m_sib = (matrix[:, j * rows : (j + 1) * rows] for j in range(3))
    cot = over_node(cot, FLIP)

    h = hb.astype(F32)
    left_hand, slopes = [], []
    for layer in range(layers):
        wa, wb, wc = w[layer]
        if layer:
            hb = h.astype(BF16)
            outer = over_node(hb, OUTER)
        sib = over_node(hb, SIBLING)
        local = mul(m_own, hb) + mul(m_sib, sib)
        first = mul(hb, wa)
        local, outer = lax.optimization_barrier((local, outer))
        mb = (local + mul(m_out, outer)).astype(BF16)
        zz = first + mul(mb, wb)
        sig = jax.nn.sigmoid(zz)
        g = (zz * sig).astype(BF16)
        slope = (sig * (1.0 + zz * (1.0 - sig))).astype(BF16)
        if layer + 1 < layers:
            h = h + mul(g, wc)
            slope = after(slope, h)
        slopes.append((slope, over_step(slope, 1)))
        left_hand += [hb, mb, g]
    cot = after(cot, left_hand[3])
    cots = (cot, over_step(cot, 1))
    n_out = over_node(m_out, OUTER)
    n_chip = jnp.concatenate([m_own, over_node(m_sib, SIBLING)], axis=0)

    own_first = (x & 1) == 1

    def of_turn(pair, turn):
        own, other = pair
        return jnp.where(own_first, other, own) if turn % 2 else jnp.where(own_first, own, other)

    upper = x >= 2
    share = width // SPLIT
    choice = feature_choice(width, x, yi, ci, width // NODES // SPLIT)
    crossing = {(0, 0): [3, 4], (1, 0): [5, 0, 1, 2]}

    def sum_rows(layer):
        pairs = [
            [jnp.where(upper, e, v) for e, v in zip(kept[turn - 2, layer], kept[turn, layer])]
            for turn in (2, 3)
        ]
        ab, dzb = [jnp.concatenate(v, axis=0) for v in zip(*pairs)]
        left = [
            jnp.concatenate([of_turn(v, turn) for turn in (2, 3)], axis=0)
            for v in lhs[3 * layer : 3 * layer + 3]
        ]
        return t_mul(jnp.concatenate(left[:2], axis=1), dzb), t_mul(left[2], ab)

    adjoint = None
    result = jnp.zeros((rows, width), F32)
    grads = [None] * layers
    kept, moving = {}, []
    for turn in range(STEPS):
        cot = of_turn(cots, turn).astype(F32)
        if turn == 0:
            adjoint = cot
        elif turn == 2:
            adjoint = cot + over_step(adjoint.astype(BF16), 3).astype(F32)
        else:
            adjoint = adjoint + cot
        for layer in range(layers - 1, -1, -1):
            wa, wb, wc = w[layer]
            ab = adjoint.astype(BF16)
            dzb = (mul_t(ab, wc) * of_turn(slopes[layer], turn).astype(F32)).astype(BF16)
            dm = mul_t(dzb, wb).astype(BF16)
            kept[turn, layer] = (ab, dzb)
            if moving:
                dm, got = lax.optimization_barrier((dm, tuple(lhs[k][1] for k in moving)))
                for k, v in zip(moving, got):
                    lhs[k][1] = v
                moving = []
            if turn == STEPS - 1 and layer == 0:
                keep, sent = split_cores(sum_rows(layer))
                grads[0] = keep + over_node(sent, SIBLING).astype(F32)
                dm = after(dm, sent)
            d_out = over_node(dm, OUTER)
            adjoint = adjoint + mul_t(dzb, wa)
            d_sib = over_node(after(dm, adjoint), SIBLING)
            if turn == 0 and layer == layers - 1:
                ordered = mul(jnp.concatenate(after(tuple(left_hand), dm), axis=0), choice).astype(BF16)
                ordered = ordered.reshape(len(left_hand), rows, width)
                lhs = [[v[:, :share], v[:, share:]] for v in ordered]
            if (turn, layer) in crossing:
                moving = crossing[turn, layer]
                joined = jnp.concatenate([after(lhs[k][1], dm) for k in moving], axis=1)
                joined = over_step(joined, 1)
                for j, k in enumerate(moving):
                    lhs[k][1] = joined[:, j * share : (j + 1) * share]
            if turn == STEPS - 1 and layer:
                kept[turn, layer] = after((ab, dzb), dm)
                keep, sent = split_cores(sum_rows(layer))
                grads[layer] = keep + over_node(sent, SIBLING).astype(F32)
            adjoint = adjoint + t_mul(n_chip, jnp.concatenate([dm, d_sib], axis=0))
            adjoint, d_out = lax.optimization_barrier((adjoint, d_out))
            adjoint = adjoint + t_mul(n_out, d_out)
        result = jnp.where(x == STEPS - 1 - turn, adjoint, result)
    result = over_node(result.astype(BF16), FLIP).astype(F32)

    grad = jnp.concatenate(grads, axis=1)
    grad_b = grad.astype(BF16)
    chunk = grad.shape[0] // Y
    total = grad[:chunk]
    for k in (2, 1, 3):
        total = total + over_node(grad_b[k * chunk : (k + 1) * chunk], y_pairs(k)).astype(F32)
    sent = total.astype(BF16).reshape(Z, chunk // Z, -1)
    got = lax.all_to_all(sent, "node", 0, 0, axis_index_groups=Z_GROUPS, tiled=False)
    mine = jnp.sum(got.astype(F32), axis=0).astype(BF16)
    beside, same, across = [over_step(mine, k).astype(F32) for k in (1, 2, 3)]
    mine, beside = mine.astype(F32) + same, beside + across
    low = jnp.where(own_first, beside, mine)
    high = jnp.where(own_first, mine, beside)
    scale = 1.0 / math.sqrt(STEPS * rows * NODES)
    return (result[None], jnp.concatenate([low, high], axis=0) * scale)


def split_cores(sums):
    both, last = sums
    share = last.shape[0]
    half = share // C
    parts = [both[:share], both[share:], last]
    keep = jnp.concatenate([v[:half] for v in parts], axis=1)
    return keep, jnp.concatenate([v[half:] for v in parts], axis=1).astype(BF16)


def solution(mesh):
    return jax.shard_map(
        on_device,
        mesh=mesh,
        in_specs=(
            P("step", "node", None),
            P("step", "node", None),
            P(),
            P("node", None, None, None),
            P("node", None),
            P("node", None),
            P("node"),
        ),
        out_specs=(P("step", "node", None), P("node", None)),
        check_vma=False,
    )
```

```python
import math

import jax
import jax.numpy as jnp
from jax import lax
from jax.sharding import PartitionSpec as P

Z, Y, C = 8, 4, 2
NODES = Z * Y * C
STEPS = 4
SPLIT = 2
F32 = jnp.float32
BF16 = jnp.bfloat16


def place(z, y, c):
    return (z * Y + y) * C + c


def split(p):
    return p // (Y * C), (p // C) % Y, p % C


def snake(p):
    z, y, c = split(p)
    return place(z, y if z % 2 == 0 else Y - 1 - y, c)


def beyond(q):
    return (q + 1) % NODES if q % 2 else (q - 1) % NODES


DEVICES = range(NODES)
FLIP = [(snake(p), p) for p in DEVICES]
OUTER = [(p, snake(beyond(snake(p)))) for p in DEVICES]
OUTER_HOME = [(beyond(snake(p)), p) for p in DEVICES]
SIBLING = [(p, p ^ 1) for p in DEVICES]
Z_GROUPS = [[place(z, y, c) for z in range(Z)] for y in range(Y) for c in range(C)]


def over_node(value, pairs):
    return lax.ppermute(value, "node", pairs)


def over_step(value, k):
    return lax.ppermute(value, "step", [(s, s ^ k) for s in range(STEPS)])


def over_both(value, k):
    pairs = [((s ^ k) * NODES + snake(p), s * NODES + p) for s in range(STEPS) for p in DEVICES]
    return lax.ppermute(value, ("step", "node"), pairs)


def y_pairs(k):
    return [(place(z, y, c), place(z, y ^ k, c)) for z in range(Z) for y in range(Y) for c in range(C)]


def mul(left, right):
    return jnp.dot(left, right, preferred_element_type=F32)


def mul_t(left, right):
    return lax.dot_general(left, right, (((1,), (1,)), ((), ())), preferred_element_type=F32)


def t_mul(left, right):
    return lax.dot_general(left, right, (((0,), (0,)), ((), ())), preferred_element_type=F32)


def assemble(tiles, sources, targets, count, core, nblk):
    slots, block = tiles.shape[0], tiles.shape[1]
    third = sources // nblk
    third = jnp.where(core == 1, 2 - third, third)
    column = third * nblk + sources % nblk
    cell = targets * (3 * nblk) + column
    live = jnp.arange(slots) < count
    hot = ((cell[None, :] == jnp.arange(3 * nblk * nblk)[:, None]) & live[None, :]).astype(BF16)
    blocks = lax.dot_general(hot, tiles, (((1,), (0,)), ((), ())), preferred_element_type=F32)
    blocks = blocks.astype(BF16).reshape(nblk, 3 * nblk, block, block)
    return blocks.transpose(0, 2, 1, 3).reshape(nblk * block, 3 * nblk * block)


def feature_choice(width, x, yi, ci, per):
    column = lax.broadcasted_iota(jnp.int32, (1, width), 1)
    row = lax.broadcasted_iota(jnp.int32, (width, 1), 0)
    row_of = column % per
    rest = column // per
    z, rest = rest % Z, rest // Z
    y, rest = rest % Y, rest // Y
    c, k = rest % C, rest // C
    feature = place(z, y ^ yi, c ^ ci) * (per * SPLIT) + ((x & 1) ^ k) * per + row_of
    return (row == feature).astype(BF16)


def after(value, *others):
    return lax.optimization_barrier((value, *others))[0]


def on_device(states, step_cotangents, weights, edge_tiles, tile_src, tile_dst, tile_counts):
    rows, width = states.shape[1], states.shape[2]
    layers = weights.shape[1] // (3 * width)
    nblk = rows // edge_tiles.shape[2]
    me = lax.axis_index("node")
    x = lax.axis_index("step")
    zi, yi, ci = split(me)
    w = [
        [weights[:, (3 * layer + j) * width : (3 * layer + j + 1) * width] for j in range(3)]
        for layer in range(layers)
    ]

    hb = over_node(states[0], FLIP)
    outer = over_node(states[0], OUTER_HOME)
    matrix = assemble(edge_tiles[0], tile_src[0], tile_dst[0], tile_counts[0], ci, nblk)
    cot = after(step_cotangents[0], matrix).astype(BF16)
    matrix = over_node(matrix, FLIP)
    m_out, m_own, m_sib = (matrix[:, j * rows : (j + 1) * rows] for j in range(3))
    cot = over_node(cot, FLIP)

    h = hb.astype(F32)
    left_hand, slopes = [], []
    for layer in range(layers):
        wa, wb, wc = w[layer]
        if layer:
            hb = h.astype(BF16)
            outer = over_node(hb, OUTER)
        sib = over_node(hb, SIBLING)
        local = mul(m_own, hb)
        first = mul(hb, wa)
        mb = (local + mul(m_sib, sib) + mul(m_out, outer)).astype(BF16)
        zz = first + mul(mb, wb)
        sig = jax.nn.sigmoid(zz)
        g = (zz * sig).astype(BF16)
        slope = (sig * (1.0 + zz * (1.0 - sig))).astype(BF16)
        if layer + 1 < layers:
            h = h + mul(g, wc)
            slope = after(slope, h)
        slopes.append((slope, over_step(slope, 1)))
        left_hand += [hb, mb, g]
    cot = after(cot, left_hand[3])
    cots = (cot, over_step(cot, 1))
    n_out = over_node(m_out, OUTER)
    n_all = jnp.concatenate([m_own, over_node(m_sib, SIBLING), n_out], axis=0)

    own_first = (x & 1) == 1

    def of_turn(pair, turn):
        own, other = pair
        return jnp.where(own_first, other, own) if turn % 2 else jnp.where(own_first, own, other)

    upper = x >= 2
    share = width // SPLIT
    choice = feature_choice(width, x, yi, ci, width // NODES // SPLIT)
    crossing = {(1, 0): [3, 4, 5, 0], (2, 0): [1, 2]}

    def sum_rows(layer):
        pairs = [
            [jnp.where(upper, e, v) for e, v in zip(kept[turn - 2, layer], kept[turn, layer])]
            for turn in (2, 3)
        ]
        ab, dzb = [jnp.concatenate(v, axis=0) for v in zip(*pairs)]
        left = [
            jnp.concatenate([of_turn(v, turn) for turn in (2, 3)], axis=0)
            for v in lhs[3 * layer : 3 * layer + 3]
        ]
        return t_mul(jnp.concatenate(left[:2], axis=1), dzb), t_mul(left[2], ab)

    adjoint = None
    result = jnp.zeros((rows, width), F32)
    grads = [None] * layers
    kept, moving = {}, []
    for turn in range(STEPS):
        cot = of_turn(cots, turn).astype(F32)
        if turn == 0:
            adjoint = cot
        elif turn == 2:
            adjoint = cot + over_step(adjoint.astype(BF16), 3).astype(F32)
        else:
            adjoint = adjoint + cot
        for layer in range(layers - 1, -1, -1):
            wa, wb, wc = w[layer]
            ab = adjoint.astype(BF16)
            dzb = (mul_t(ab, wc) * of_turn(slopes[layer], turn).astype(F32)).astype(BF16)
            dm = mul_t(dzb, wb).astype(BF16)
            kept[turn, layer] = (ab, dzb)
            if moving:
                dm, got = lax.optimization_barrier((dm, tuple(lhs[k][1] for k in moving)))
                for k, v in zip(moving, got):
                    lhs[k][1] = v
                moving = []
            if turn == STEPS - 1 and layer == 0:
                keep, sent = split_cores(sum_rows(layer))
                grads[0] = keep + over_node(sent, SIBLING).astype(F32)
                dm = after(dm, sent)
            d_out = over_node(dm, OUTER)
            adjoint = adjoint + mul_t(dzb, wa)
            d_sib = over_node(after(dm, adjoint), SIBLING)
            if turn == 0 and layer == layers - 1:
                ordered = mul(jnp.concatenate(after(tuple(left_hand), dm), axis=0), choice).astype(BF16)
                ordered = ordered.reshape(len(left_hand), rows, width)
                lhs = [[v[:, :share], v[:, share:]] for v in ordered]
            if (turn, layer) in crossing:
                moving = crossing[turn, layer]
                joined = jnp.concatenate([after(lhs[k][1], dm) for k in moving], axis=1)
                joined = over_step(joined, 1)
                for j, k in enumerate(moving):
                    lhs[k][1] = joined[:, j * share : (j + 1) * share]
            if turn == STEPS - 1 and layer:
                kept[turn, layer] = after((ab, dzb), dm)
                keep, sent = split_cores(sum_rows(layer))
                grads[layer] = keep + over_node(sent, SIBLING).astype(F32)
            adjoint = adjoint + t_mul(n_all, jnp.concatenate([dm, d_sib, d_out], axis=0))
        result = jnp.where(x == STEPS - 1 - turn, adjoint, result)
    result = over_node(result.astype(BF16), FLIP).astype(F32)

    grad = jnp.concatenate(grads, axis=1)
    grad_b = grad.astype(BF16)
    chunk = grad.shape[0] // Y
    total = grad[:chunk]
    for k in (2, 1, 3):
        total = total + over_node(grad_b[k * chunk : (k + 1) * chunk], y_pairs(k)).astype(F32)
    sent = total.astype(BF16).reshape(Z, chunk // Z, -1)
    got = lax.all_to_all(sent, "node", 0, 0, axis_index_groups=Z_GROUPS, tiled=False)
    mine = jnp.sum(got.astype(F32), axis=0).astype(BF16)
    beside, same, across = [over_step(mine, k).astype(F32) for k in (1, 2, 3)]
    mine, beside = mine.astype(F32) + same, beside + across
    low = jnp.where(own_first, beside, mine)
    high = jnp.where(own_first, mine, beside)
    scale = 1.0 / math.sqrt(STEPS * rows * NODES)
    return (result[None], jnp.concatenate([low, high], axis=0) * scale)


def split_cores(sums):
    both, last = sums
    share = last.shape[0]
    half = share // C
    parts = [both[:share], both[share:], last]
    keep = jnp.concatenate([v[:half] for v in parts], axis=1)
    return keep, jnp.concatenate([v[half:] for v in parts], axis=1).astype(BF16)


def solution(mesh):
    return jax.shard_map(
        on_device,
        mesh=mesh,
        in_specs=(
            P("step", "node", None),
            P("step", "node", None),
            P(),
            P("node", None, None, None),
            P("node", None),
            P("node", None),
            P("node"),
        ),
        out_specs=(P("step", "node", None), P("node", None)),
        check_vma=False,
    )
```
